512 devices in a mesh: tm: 64 (over z, y_lo, core), sta: 8 (over x, y_hi).
Axes of the slice: x: 4, y: 4 (y_hi: 2, y_lo: 2; y = y_hi * 2 + y_lo), z: 16, core: 2. Of those that a mesh axis runs over, the one named last changes fastest.
Arguments:
- traces: float32 [48, 32768], P('sta', 'tm'), may hold values from -200 to 200
- bandpass_taps: float32 [128], replicated, may hold values from -0.5 to 0.5
- templates: bfloat16 [256, 48, 400], P(None, 'sta'), may hold values from -6 to 6
- moveouts: int32 [256, 48], P(None, 'sta'), may hold values from 0 to 400, as said below
- station_mask: int32 [16], P('sta'), may hold values 0 or 1
Outputs:
- network_stack: float32 [256, 32768], P('sta', 'tm')
The draws below stay inside these ranges and needn't reach their ends.
Inputs may be any that keep to these rules, and one draw needn't show every extreme that they name: `moveouts`: every template has offset 0 on some channel and 400 on another.
All inputs are finite; a program needn't handle non-finite values. No bound on the sum of `station_mask` on one device may be relied on, other than what follows from the above.
Results may differ from the reference program's by a relative error of at most 0.0041.
Values sent between devices are 32-bit elements; how exact they have to be, the bound alone decides.
A program may use at most 64 MiB of HBM per device.

```python
import math
import jax
import jax.numpy as jnp
from jax import lax

TEMPLATES = 256
TLEN = 400
DMAX = 400
NTAP = 128
STATIONS = 16
CHANNELS = 48
NT = 32768


def draw_traces(key, part):
    key = jax.random.fold_in(key, 11)
    key_noise, key_row, key_envelope = jax.random.split(key, 3)
    shape = (CHANNELS, NT)
    noise = jnp.clip(jax.random.normal(key_noise, shape, jnp.float32), -6.0, 6.0)
    row_level = jax.random.uniform(key_row, (CHANNELS, 1), jnp.float32, 0.0, 1.0)
    envelope = jax.random.uniform(key_envelope, (CHANNELS, NT // 32), jnp.float32, 0.0, 1.0)
    envelope = jnp.repeat(envelope, 32, axis=1)
    return noise * jnp.exp(math.log(10.0) * (0.5 * row_level + envelope))


def draw_moveouts(key, part):
    key = jax.random.fold_in(key, 5)
    key_base, key_low, key_step = jax.random.split(key, 3)
    base = jax.random.randint(key_base, (TEMPLATES, CHANNELS), 0, DMAX + 1, dtype=jnp.int32)
    lowest = jax.random.randint(key_low, (TEMPLATES, 1), 0, CHANNELS, dtype=jnp.int32)
    offset = jax.random.randint(key_step, (TEMPLATES, 1), 1, CHANNELS, dtype=jnp.int32)
    highest = (lowest + offset) % CHANNELS
    column = jnp.arange(CHANNELS, dtype=jnp.int32)[None, :]
    return jnp.where(column == lowest, 0, jnp.where(column == highest, DMAX, base)).astype(jnp.int32)


def with_ends(entries, own_key, smallest, top_value):
    longest = entries.shape.index(max(entries.shape))
    spots = []
    for shift in (0, 1):
        where = [jax.random.randint(jax.random.fold_in(own_key, axis), (), 0, length) for axis, length in enumerate(entries.shape)]
        where[longest] = (where[longest] + shift) % entries.shape[longest]
        spots.append(tuple(where))
    return entries.at[spots[0]].set(smallest).at[spots[1]].set(top_value)


def block_scale(stream_key, extent, cuts, low, high):
    factor_of, own = 1.0, jax.random.fold_in(stream_key, 6)
    for dim, parts in cuts:
        draws = jnp.exp(jax.random.uniform(jax.random.fold_in(own, dim), (parts,), jnp.float32, low / len(cuts), high / len(cuts)))
        factor_of = factor_of * jnp.repeat(draws, extent[dim] // parts).reshape([-1 if axis == dim else 1 for axis in range(len(extent))])
    return factor_of


def scatter_about(own_key, shape, scale, bound, shards=(), kind=jnp.bfloat16):
    level = block_scale(own_key, shape, shards, -0.22, 0.18) if shards else 1.0
    array = jax.random.normal(own_key, shape, jnp.float32) * scale * level
    return jnp.minimum(jnp.maximum(array, -bound), bound).astype(kind)


def setup_inputs(seed: int = 0) -> dict:
    streams_of = jax.random.split(jax.random.key(seed), 6)
    traces = draw_traces(jax.random.fold_in(streams_of[5], 71), 0)
    bandpass_taps = scatter_about(streams_of[1], (NTAP,), NTAP ** -0.5, 0.5, (), jnp.float32)
    templates = scatter_about(streams_of[2], (TEMPLATES, CHANNELS, TLEN), 1.0, 6.0, ((1, 8),))
    moveouts = draw_moveouts(jax.random.fold_in(streams_of[5], 71), 0)
    station_mask = with_ends((jax.random.randint(streams_of[4], (STATIONS,), 0, 5) < 4).astype(jnp.int32), jax.random.fold_in(streams_of[4], 1), 0, 1)
    return dict(traces=traces, bandpass_taps=bandpass_taps, templates=templates, moveouts=moveouts, station_mask=station_mask)


def bandpass_all(traces, bandpass_taps):
    length = NT + NTAP
    spectrum = jnp.fft.rfft(traces, n=length, axis=1) * jnp.fft.rfft(bandpass_taps, n=length)[None, :]
    return jnp.fft.irfft(spectrum, n=length, axis=1)[:, :NT].astype(jnp.float32)

def unit_templates(templates):
    values = templates.astype(jnp.float32)
    centred = values - lax.optimization_barrier(jnp.mean(values, axis=-1, keepdims=True))
    factor = lax.rsqrt(lax.optimization_barrier(jnp.mean(centred * centred, axis=-1, keepdims=True)) + 1e-06) * (1.0 / math.sqrt(TLEN))
    return (centred * factor).astype(jnp.bfloat16)

def reference(traces, bandpass_taps, templates, moveouts, station_mask):
    filtered = bandpass_all(traces, bandpass_taps)
    unit = unit_templates(templates)
    available = jnp.repeat(station_mask, 3).astype(jnp.float32)
    offsets = jnp.arange(TLEN, dtype=jnp.int32)[:, None] + jnp.arange(NT, dtype=jnp.int32)[None, :]
    times = jnp.arange(NT, dtype=jnp.int32)

    def add_channel(network, inputs):
        signal, kernel, delays, weight = inputs
        padded = jnp.concatenate([signal, jnp.zeros((TLEN,), jnp.float32)])
        windows = padded[offsets]
        window_sum = lax.optimization_barrier(jnp.sum(windows, axis=0))
        window_power = lax.optimization_barrier(jnp.sum(windows * windows, axis=0))
        inverse_norm = lax.rsqrt(jnp.maximum(window_power - window_sum * window_sum / TLEN, 1.0))
        rounded = lax.optimization_barrier(windows.astype(jnp.bfloat16)).astype(jnp.float32)
        products = jnp.dot(kernel.astype(jnp.float32), rounded, precision=lax.Precision.HIGHEST)
        correlation = products * inverse_norm[None, :]
        positions = times[None, :] + delays[:, None]
        in_range = positions < NT
        moved = jnp.take_along_axis(correlation, jnp.minimum(positions, NT - 1).astype(jnp.int32), axis=1)
        return (network + jnp.where(in_range, moved, 0.0) * weight, None)
    start = jnp.zeros((TEMPLATES, NT), jnp.float32)
    network, unused = lax.scan(add_channel, start, (filtered, jnp.transpose(unit, (1, 0, 2)), jnp.transpose(moveouts), available))
    return network
```

```python
import functools
import math

import jax
import jax.numpy as jnp
from jax import lax
from jax.experimental import pallas as pl
from jax.experimental.pallas import tpu as pltpu
from jax.sharding import PartitionSpec as P

TLEN = 400
DMAX = 400
LANE = 128
MESH = pl.DeviceIdType.MESH


def shifted_left(values, step):
    extent = values.shape[-1]
    if step % LANE == 0:
        return jnp.concatenate([values[:, step:], values[:, :step]], axis=1)
    return pltpu.roll(values, extent - step, 1)


def toeplitz(taps):
    rows = jnp.broadcast_to(taps, (LANE, LANE))
    turned = pltpu.roll(rows, 0, 1, stride=1, stride_axis=0)
    row = lax.broadcasted_iota(jnp.int32, (LANE, LANE), 0)
    lane = lax.broadcasted_iota(jnp.int32, (LANE, LANE), 1)
    below = jnp.where(lane >= row, turned, 0.0)
    above = jnp.where(lane < row, turned, 0.0)
    return jnp.concatenate([above, below], axis=0)


def kernel(
    sizes,
    traces_ref,
    taps_ref,
    templates_ref,
    moveouts_ref,
    mask_ref,
    out_ref,
    window,
    raw_templates,
    unit,
    hankel,
    partial,
    received,
    template_sem,
    halo_send,
    halo_recv,
    sum_send,
    sum_recv,
):
    tm_count, sta_count, slab, channels, share = sizes
    x_count = sta_count // 2
    kcount = share * sta_count
    me_t = lax.axis_index("tm")
    me_s = lax.axis_index("sta")
    my_x, my_y = me_s // 2, lax.rem(me_s, 2)

    def time_device(by):
        return lax.rem(me_t + by + tm_count, tm_count)

    def station_device(dx, dy):
        return 2 * lax.rem(my_x + dx, x_count) + lax.rem(my_y + dy, 2)

    offsets = [(dx, dy) for dx in range(x_count) for dy in range(2) if (dx, dy) != (0, 0)]

    barrier = pltpu.get_barrier_semaphore()
    for by in (-2, -1, 1, 2):
        pl.semaphore_signal(
            barrier, inc=1, device_id={"tm": time_device(by)}, device_id_type=MESH
        )
    for dx, dy in offsets:
        pl.semaphore_signal(
            barrier, inc=1, device_id={"sta": station_device(dx, dy)}, device_id_type=MESH
        )
    fetch = pltpu.make_async_copy(templates_ref, raw_templates, template_sem)
    fetch.start()

    window[0:channels, LANE : LANE + slab] = traces_ref[...]
    window[channels:8, LANE : LANE + slab] = jnp.zeros((8 - channels, slab), jnp.float32)
    bands = toeplitz(taps_ref[...])
    pl.semaphore_wait(barrier, 4 + len(offsets))

    def halo(slot, by, src, dst, width):
        return pltpu.make_async_remote_copy(
            src_ref=window.at[:, pl.ds(src, width)],
            dst_ref=window.at[:, pl.ds(dst, width)],
            send_sem=halo_send.at[slot],
            recv_sem=halo_recv.at[slot],
            device_id={"tm": time_device(by)},
            device_id_type=MESH,
        )

    rest = 11 * LANE + LANE - (LANE + 2 * slab)
    halos = [
        halo(0, -2, LANE, LANE + 2 * slab, rest),
        halo(1, -1, LANE, LANE + slab, slab),
        halo(2, 1, slab, 0, LANE),
    ]
    for copy in halos:
        copy.start()

    fetch.wait()
    for c in range(channels):
        values = raw_templates[c].astype(jnp.float32)
        mean = jnp.sum(values, axis=0, keepdims=True) * (1.0 / TLEN)
        centred = values - mean
        power = jnp.sum(centred * centred, axis=0, keepdims=True) * (1.0 / TLEN)
        factor = lax.rsqrt(power + 1e-06) * (1.0 / math.sqrt(TLEN))
        scaled = centred * factor
        padded = jnp.concatenate(
            [scaled, jnp.zeros((512 - TLEN, kcount), jnp.float32)], axis=0
        )
        unit[c] = jnp.transpose(padded).astype(jnp.bfloat16)
    delays = jnp.transpose(
        jnp.concatenate(
            [moveouts_ref[...], jnp.zeros((8 - channels, kcount), jnp.int32)], axis=0
        )
    )

    for copy in halos:
        copy.wait()

    first = jnp.where(me_t == 0, 0.0, window[:, 0:LANE])
    raw = [first] + [window[:, LANE * b : LANE * (b + 1)] for b in range(1, 12)]
    lows = jnp.concatenate(raw[:11], axis=0)
    highs = jnp.concatenate(raw[1:], axis=0)
    filtered = jnp.dot(
        jnp.concatenate([lows, highs], axis=1),
        bands,
        precision=lax.Precision.HIGHEST,
        preferred_element_type=jnp.float32,
    )
    remaining = (tm_count - me_t) * slab
    blocks = [
        jnp.where(b * LANE < remaining, filtered[8 * b : 8 * b + 8], 0.0) for b in range(11)
    ]
    series = jnp.concatenate(blocks, axis=1)

    level = jnp.concatenate([series, series * series], axis=0)
    kept = {}
    for bit in range(9):
        if bit in (4, 7, 8):
            kept[bit] = level
        if bit < 8:
            level = level + shifted_left(level, 1 << bit)
    sums = kept[8] + shifted_left(kept[7], 256) + shifted_left(kept[4], 384)
    window_sum, window_power = sums[0:8, : 8 * LANE], sums[8:16, : 8 * LANE]
    inverse_norm = lax.rsqrt(
        jnp.maximum(window_power - window_sum * window_sum * (1.0 / TLEN), 1.0)
    )
    row = lax.broadcasted_iota(jnp.int32, (8, 8 * LANE), 0)
    weight = jnp.where(row < 3, mask_ref[0], mask_ref[1]).astype(jnp.float32)
    inverse_norm = inverse_norm * weight

    lane = lax.broadcasted_iota(jnp.int32, (LANE, LANE), 1)
    line = lax.broadcasted_iota(jnp.int32, (LANE, LANE), 0)
    inside = lane + line < LANE
    turn = lax.rem(lane + line, LANE)
    for c in range(channels):
        turned = [
            jnp.take_along_axis(
                jnp.broadcast_to(blocks[b][c : c + 1], (LANE, LANE)),
                turn,
                axis=1,
                mode="promise_in_bounds",
            )
            for b in range(11)
        ]
        turned.append(jnp.zeros((LANE, LANE), jnp.float32))
        for b in range(11):
            hankel[c, :, LANE * b : LANE * (b + 1)] = jnp.where(
                inside, turned[b], turned[b + 1]
            ).astype(jnp.bfloat16)

    lane_k = lax.broadcasted_iota(jnp.int32, (kcount, LANE), 1)
    total = [jnp.zeros((kcount, LANE), jnp.float32) for _ in range(4)]
    for c in range(channels):
        matrix = jnp.concatenate(
            [hankel[c, :, LANE * m : LANE * (m + 8)] for m in range(4)], axis=0
        )
        products = jnp.dot(unit[c], matrix, preferred_element_type=jnp.float32)
        delay = jnp.broadcast_to(delays[:, c : c + 1], (kcount, LANE))
        by_256 = delay >= 256
        by_128 = lax.rem(delay, 256) >= 128
        fine = lax.rem(delay, 128)
        p = [
            products[:, LANE * b : LANE * (b + 1)] * inverse_norm[c : c + 1, LANE * b : LANE * (b + 1)]
            for b in range(8)
        ]
        p = [jnp.where(by_256, p[b + 2], p[b]) for b in range(6)]
        p = [jnp.where(by_128, p[b + 1], p[b]) for b in range(5)]
        source = lax.rem(lane_k + fine, LANE)
        ahead = lane_k < fine
        for b in range(4):
            joined = jnp.where(ahead, p[b + 1], p[b])
            total[b] = total[b] + jnp.take_along_axis(
                joined, source, axis=1, mode="promise_in_bounds"
            )
    for b in range(4):
        partial[:, LANE * b : LANE * (b + 1)] = total[b]

    copies = []
    for slot, (dx, dy) in enumerate(offsets):
        peer = station_device(dx, dy)
        copy = pltpu.make_async_remote_copy(
            src_ref=partial.at[pl.ds(pl.multiple_of(peer * share, share), share)],
            dst_ref=received.at[slot],
            send_sem=sum_send.at[slot],
            recv_sem=sum_recv.at[slot],
            device_id={"sta": peer},
            device_id_type=MESH,
        )
        copy.start()
        copies.append(copy)
    result = partial[pl.ds(pl.multiple_of(me_s * share, share), share), :]
    for slot, copy in enumerate(copies):
        copy.wait()
        result = result + received[slot]
    out_ref[...] = result


def per_device(sizes, traces, taps, templates, moveouts, mask):
    tm_count, sta_count, slab, channels, share = sizes
    kcount = share * sta_count
    vmem = pl.BlockSpec(memory_space=pltpu.VMEM)
    return pl.pallas_call(
        functools.partial(kernel, sizes),
        out_shape=jax.ShapeDtypeStruct((share, slab), jnp.float32),
        in_specs=[
            vmem,
            vmem,
            pl.BlockSpec(memory_space=pl.ANY),
            vmem,
            pl.BlockSpec(memory_space=pltpu.SMEM),
        ],
        out_specs=vmem,
        scratch_shapes=[
            pltpu.VMEM((8, 12 * LANE), jnp.float32),
            pltpu.VMEM((channels, TLEN, kcount), jnp.bfloat16),
            pltpu.VMEM((channels, kcount, 512), jnp.bfloat16),
            pltpu.VMEM((channels, LANE, 11 * LANE), jnp.bfloat16),
            pltpu.VMEM((kcount, slab), jnp.float32),
            pltpu.VMEM((sta_count - 1, share, slab), jnp.float32),
            pltpu.SemaphoreType.DMA,
            pltpu.SemaphoreType.DMA((3,)),
            pltpu.SemaphoreType.DMA((3,)),
            pltpu.SemaphoreType.DMA((sta_count - 1,)),
            pltpu.SemaphoreType.DMA((sta_count - 1,)),
        ],
        compiler_params=pltpu.CompilerParams(
            collective_id=0, has_side_effects=True, vmem_limit_bytes=48 * 2**20
        ),
        cost_estimate=pl.CostEstimate(
            flops=2 * kcount * channels * 512 * 1024, bytes_accessed=4 * 2**20, transcendentals=0
        ),
        name="network_match",
    )(
        traces,
        taps.reshape(1, LANE),
        jnp.transpose(templates, (1, 2, 0)),
        jnp.transpose(moveouts),
        mask,
    )


def solution(mesh):
    tm_count, sta_count = mesh.shape["tm"], mesh.shape["sta"]

    def run(traces, taps, templates, moveouts, mask):
        sizes = (
            tm_count,
            sta_count,
            traces.shape[1] // tm_count,
            traces.shape[0] // sta_count,
            templates.shape[0] // sta_count,
        )
        return jax.shard_map(
            functools.partial(per_device, sizes),
            mesh=mesh,
            in_specs=(P("sta", "tm"), P(), P(None, "sta", None), P(None, "sta"), P("sta")),
            out_specs=P("sta", "tm"),
            check_vma=False,
        )(traces, taps, templates, moveouts, mask)

    return run
```

```python
import functools
import math

import jax
import jax.numpy as jnp
from jax import lax
from jax.experimental import pallas as pl
from jax.experimental.pallas import tpu as pltpu
from jax.sharding import PartitionSpec as P

TLEN = 400
DMAX = 400
LANE = 128
BLOCKS = 11
CHUNKS = (4, 4)
MESH = pl.DeviceIdType.MESH


def shifted_left(values, step):
    extent = values.shape[-1]
    if step % LANE == 0:
        return jnp.concatenate([values[:, step:], values[:, :step]], axis=1)
    return pltpu.roll(values, extent - step, 1)


def toeplitz(taps):
    rows = jnp.broadcast_to(taps, (LANE, LANE))
    turned = pltpu.roll(rows, 0, 1, stride=1, stride_axis=0)
    row = lax.broadcasted_iota(jnp.int32, (LANE, LANE), 0)
    lane = lax.broadcasted_iota(jnp.int32, (LANE, LANE), 1)
    below = jnp.where(lane >= row, turned, 0.0)
    above = jnp.where(lane < row, turned, 0.0)
    return jnp.concatenate([above, below], axis=0)


def position():
    return lax.axis_index("tm"), lax.axis_index("sta")


class Places:
    def __init__(self, sizes):
        self.tm_count, self.sta_count = sizes[0], sizes[1]
        self.x_count = self.sta_count // 2
        self.me_t, self.me_s = position()
        self.offsets = [
            (dx, dy) for dx in range(self.x_count) for dy in range(2) if (dx, dy) != (0, 0)
        ]

    def time_device(self, by):
        return lax.rem(self.me_t + by + self.tm_count, self.tm_count)

    def station_device(self, dx, dy):
        x = lax.rem(self.me_s // 2 + dx, self.x_count)
        return 2 * x + lax.rem(lax.rem(self.me_s, 2) + dy, 2)


def greet(places):
    barrier = pltpu.get_barrier_semaphore()
    for by in (-2, -1, 1, 2):
        pl.semaphore_signal(
            barrier, inc=1, device_id={"tm": places.time_device(by)}, device_id_type=MESH
        )
    for dx, dy in places.offsets:
        pl.semaphore_signal(
            barrier, inc=1, device_id={"sta": places.station_device(dx, dy)}, device_id_type=MESH
        )


def await_greetings(places):
    pl.semaphore_wait(pltpu.get_barrier_semaphore(), 4 + len(places.offsets))


def start_halo(places, slab, window, halo_send, halo_recv):
    def halo(slot, by, src, dst, width):
        return pltpu.make_async_remote_copy(
            src_ref=window.at[:, pl.ds(src, width)],
            dst_ref=window.at[:, pl.ds(dst, width)],
            send_sem=halo_send.at[slot],
            recv_sem=halo_recv.at[slot],
            device_id={"tm": places.time_device(by)},
            device_id_type=MESH,
        )

    rest = (BLOCKS + 1) * LANE - (LANE + 2 * slab)
    halos = [
        halo(0, -2, LANE, LANE + 2 * slab, rest),
        halo(1, -1, LANE, LANE + slab, slab),
        halo(2, 1, slab, 0, LANE),
    ]
    for copy in halos:
        copy.start()
    return halos


def await_halo(halos):
    for copy in halos:
        copy.wait()


def prepare_template(values):
    values = values.astype(jnp.float32)
    mean = jnp.sum(values, axis=0, keepdims=True) * (1.0 / TLEN)
    centred = values - mean
    power = jnp.sum(centred * centred, axis=0, keepdims=True) * (1.0 / TLEN)
    factor = lax.rsqrt(power + 1e-06) * (1.0 / math.sqrt(TLEN))
    scaled = centred * factor
    return jnp.transpose(scaled).astype(jnp.bfloat16)


def prepare_templates(raw_templates, unit):
    for c in range(unit.shape[0]):
        unit[c] = prepare_template(raw_templates[c])


def bandpass(places, slab, window, bands):
    first = jnp.where(places.me_t == 0, 0.0, window[:, 0:LANE])
    raw = [first] + [window[:, LANE * b : LANE * (b + 1)] for b in range(1, BLOCKS + 1)]
    lows = jnp.concatenate(raw[:BLOCKS], axis=0)
    highs = jnp.concatenate(raw[1:], axis=0)
    filtered = jnp.dot(
        jnp.concatenate([lows, highs], axis=1),
        bands,
        precision=lax.Precision.HIGHEST,
        preferred_element_type=jnp.float32,
    )
    remaining = (places.tm_count - places.me_t) * slab
    return [
        jnp.where(b * LANE < remaining, filtered[8 * b : 8 * b + 8], 0.0) for b in range(BLOCKS)
    ]


def window_norm(blocks, mask):
    series = jnp.concatenate(blocks, axis=1)
    level = jnp.concatenate([series, series * series], axis=0)
    kept = {}
    for bit in range(9):
        if bit in (4, 7, 8):
            kept[bit] = level
        if bit < 8:
            level = level + shifted_left(level, 1 << bit)
    sums = kept[8] + shifted_left(kept[7], 256) + shifted_left(kept[4], 384)
    window_sum, window_power = sums[0:8, : 8 * LANE], sums[8:16, : 8 * LANE]
    inverse_norm = lax.rsqrt(
        jnp.maximum(window_power - window_sum * window_sum * (1.0 / TLEN), 1.0)
    )
    row = lax.broadcasted_iota(jnp.int32, (8, 8 * LANE), 0)
    return inverse_norm * jnp.where(row < 3, mask[0], mask[1]).astype(jnp.float32)


def build_hankel(blocks, hankel):
    lane = lax.broadcasted_iota(jnp.int32, (LANE, LANE), 1)
    line = lax.broadcasted_iota(jnp.int32, (LANE, LANE), 0)
    inside = lane + line < LANE
    turn = lax.rem(lane + line, LANE)
    for c in range(hankel.shape[0]):
        turned = [
            jnp.take_along_axis(
                jnp.broadcast_to(blocks[b][c : c + 1], (LANE, LANE)),
                turn,
                axis=1,
                mode="promise_in_bounds",
            )
            for b in range(BLOCKS)
        ]
        turned.append(jnp.zeros((LANE, LANE), jnp.float32))
        for b in range(BLOCKS):
            hankel[c, :, LANE * b : LANE * (b + 1)] = jnp.where(
                inside, turned[b], turned[b + 1]
            ).astype(jnp.bfloat16)


def correlate(c, rows, unit, hankel):
    matrix = jnp.concatenate(
        [
            hankel[c, 0 : min(LANE, TLEN - LANE * m), LANE * m : LANE * (m + 8)]
            for m in range(4)
        ],
        axis=0,
    )
    return jnp.dot(rows, matrix, preferred_element_type=jnp.float32)


def moved(products, inverse_norm, delay):
    rows = products.shape[0]
    lane = lax.broadcasted_iota(jnp.int32, (rows, LANE), 1)
    by_256 = delay >= 256
    by_128 = lax.rem(delay, 256) >= 128
    fine = lax.rem(delay, 128)
    p = [
        products[:, LANE * b : LANE * (b + 1)] * inverse_norm[:, LANE * b : LANE * (b + 1)]
        for b in range(8)
    ]
    p = [jnp.where(by_256, p[b + 2], p[b]) for b in range(6)]
    p = [jnp.where(by_128, p[b + 1], p[b]) for b in range(5)]
    source = lax.rem(lane + fine, LANE)
    ahead = lane < fine
    return [
        jnp.take_along_axis(
            jnp.where(ahead, p[b + 1], p[b]), source, axis=1, mode="promise_in_bounds"
        )
        for b in range(4)
    ]


def match(peers, share, delays, inverse_norm, unit, hankel, partial):
    count = len(peers) * share
    starts = [pl.multiple_of(peer * share, share) for peer in peers]
    total = None
    for c in range(unit.shape[0]):
        rows = jnp.concatenate([unit[c, pl.ds(start, share), :] for start in starts], axis=0)
        products = correlate(c, rows, unit, hankel)
        delay = jnp.concatenate([delays[pl.ds(start, share), c : c + 1] for start in starts], axis=0)
        terms = moved(products, inverse_norm[c : c + 1], jnp.broadcast_to(delay, (count, LANE)))
        total = terms if total is None else [a + b for a, b in zip(total, terms)]
    for i, start in enumerate(starts):
        for b in range(4):
            partial[pl.ds(start, share), LANE * b : LANE * (b + 1)] = total[b][
                share * i : share * (i + 1)
            ]


def send_sum(places, share, slot, peer, partial, received, sum_send, sum_recv):
    copy = pltpu.make_async_remote_copy(
        src_ref=partial.at[pl.ds(pl.multiple_of(peer * share, share), share)],
        dst_ref=received.at[slot],
        send_sem=sum_send.at[slot],
        recv_sem=sum_recv.at[slot],
        device_id={"sta": peer},
        device_id_type=MESH,
    )
    copy.start()
    return copy


def add_received(places, share, copies, partial, received, out_ref):
    result = partial[pl.ds(pl.multiple_of(places.me_s * share, share), share), :]
    for slot, copy in copies:
        copy.wait()
        result = result + received[slot]
    out_ref[...] = result


def chunks_of(places):
    far = sorted(places.offsets, key=lambda o: -(min(o[0], places.x_count - o[0]) + 2 * o[1]))
    far.append((0, 0))
    groups = [far[sum(CHUNKS[:i]) : sum(CHUNKS[: i + 1])] for i in range(len(CHUNKS))]
    return [group for group in groups if group]


def kernel(
    sizes,
    traces_ref,
    taps_ref,
    templates_ref,
    moveouts_ref,
    mask_ref,
    out_ref,
    samples,
    taps,
    moveouts,
    mask,
    window,
    raw_templates,
    unit,
    delays,
    hankel,
    partial,
    received,
    local_sem,
    halo_send,
    halo_recv,
    sum_send,
    sum_recv,
):
    slab, channels, share = sizes[2:]
    kcount = share * sizes[1]
    places = Places(sizes)
    fetches = [
        pltpu.make_async_copy(src, dst, local_sem.at[i])
        for i, (src, dst) in enumerate(
            [(traces_ref, samples), (taps_ref, taps), (moveouts_ref, moveouts), (mask_ref, mask)]
            + [(templates_ref.at[c], raw_templates.at[c]) for c in range(channels)]
        )
    ]
    for fetch in fetches:
        fetch.start()
    greet(places)
    fetches[0].wait()
    window[0:channels, LANE : LANE + slab] = samples[...]
    window[channels:8, LANE : LANE + slab] = jnp.zeros((8 - channels, slab), jnp.float32)
    await_greetings(places)
    halos = start_halo(places, slab, window, halo_send, halo_recv)
    fetches[1].wait()
    bands = toeplitz(taps[...])
    fetches[2].wait()
    delays[:, 0:8] = jnp.transpose(
        jnp.concatenate([moveouts[...], jnp.zeros((8 - channels, kcount), jnp.int32)], axis=0)
    )
    for fetch in fetches[3:]:
        fetch.wait()
    prepare_templates(raw_templates, unit)
    await_halo(halos)
    blocks = bandpass(places, slab, window, bands)
    inverse_norm = window_norm(blocks, mask)
    build_hankel(blocks, hankel)
    copies = []
    for chunk in chunks_of(places):
        peers = [places.station_device(dx, dy) for dx, dy in chunk]
        match(peers, share, delays, inverse_norm, unit, hankel, partial)
        for offset, peer in zip(chunk, peers):
            if offset != (0, 0):
                slot = places.offsets.index(offset)
                copy = send_sum(places, share, slot, peer, partial, received, sum_send, sum_recv)
                copies.append((slot, copy))
    add_received(places, share, copies, partial, received, out_ref)


def per_device(sizes, traces, taps, templates, moveouts, mask):
    tm_count, sta_count, slab, channels, share = sizes
    kcount = share * sta_count
    vmem = pl.BlockSpec(memory_space=pltpu.VMEM)
    hbm = pl.BlockSpec(memory_space=pltpu.HBM)
    return pl.pallas_call(
        functools.partial(kernel, sizes),
        out_shape=jax.ShapeDtypeStruct((share, slab), jnp.float32),
        in_specs=[hbm] * 5,
        out_specs=vmem,
        scratch_shapes=[
            pltpu.VMEM((channels, slab), jnp.float32),
            pltpu.VMEM((1, LANE), jnp.float32),
            pltpu.VMEM((channels, kcount), jnp.int32),
            pltpu.SMEM((2,), jnp.int32),
            pltpu.VMEM((8, (BLOCKS + 1) * LANE), jnp.float32),
            pltpu.VMEM((channels, TLEN, kcount), jnp.bfloat16),
            pltpu.VMEM((channels, kcount, TLEN), jnp.bfloat16),
            pltpu.VMEM((kcount, LANE), jnp.int32),
            pltpu.VMEM((channels, LANE, BLOCKS * LANE), jnp.bfloat16),
            pltpu.VMEM((kcount, slab), jnp.float32),
            pltpu.VMEM((sta_count - 1, share, slab), jnp.float32),
            pltpu.SemaphoreType.DMA((4 + channels,)),
            pltpu.SemaphoreType.DMA((3,)),
            pltpu.SemaphoreType.DMA((3,)),
            pltpu.SemaphoreType.DMA((sta_count - 1,)),
            pltpu.SemaphoreType.DMA((sta_count - 1,)),
        ],
        compiler_params=pltpu.CompilerParams(
            collective_id=0, has_side_effects=True, vmem_limit_bytes=24 * 2**20
        ),
        cost_estimate=pl.CostEstimate(
            flops=2 * kcount * channels * 512 * 1024, bytes_accessed=4 * 2**20, transcendentals=0
        ),
        name="network_match",
    )(
        *(
            pltpu.with_memory_space_constraint(array, pltpu.HBM)
            for array in (
                traces,
                taps.reshape(1, LANE),
                jnp.transpose(templates, (1, 2, 0)),
                jnp.transpose(moveouts),
                mask,
            )
        )
    )


def solution(mesh):
    tm_count, sta_count = mesh.shape["tm"], mesh.shape["sta"]

    def run(traces, taps, templates, moveouts, mask):
        sizes = (
            tm_count,
            sta_count,
            traces.shape[1] // tm_count,
            traces.shape[0] // sta_count,
            templates.shape[0] // sta_count,
        )
        return jax.shard_map(
            functools.partial(per_device, sizes),
            mesh=mesh,
            in_specs=(P("sta", "tm"), P(), P(None, "sta", None), P(None, "sta"), P("sta")),
            out_specs=P("sta", "tm"),
            check_vma=False,
        )(traces, taps, templates, moveouts, mask)

    return run
```

```python
import functools
import math

import jax
import jax.numpy as jnp
from jax import lax
from jax.experimental import pallas as pl
from jax.experimental.pallas import tpu as pltpu
from jax.sharding import PartitionSpec as P

TLEN = 400
DMAX = 400
LANE = 128
BLOCKS = 11
CHUNKS = (4, 4)
MESH = pl.DeviceIdType.MESH


def shifted_left(values, step):
    extent = values.shape[-1]
    if step % LANE == 0:
        return jnp.concatenate([values[:, step:], values[:, :step]], axis=1)
    return pltpu.roll(values, extent - step, 1)


def toeplitz(taps):
    rows = jnp.broadcast_to(taps, (LANE, LANE))
    turned = pltpu.roll(rows, 0, 1, stride=1, stride_axis=0)
    row = lax.broadcasted_iota(jnp.int32, (LANE, LANE), 0)
    lane = lax.broadcasted_iota(jnp.int32, (LANE, LANE), 1)
    below = jnp.where(lane >= row, turned, 0.0)
    above = jnp.where(lane < row, turned, 0.0)
    return jnp.concatenate([above, below], axis=0)


def position():
    return lax.axis_index("tm"), lax.axis_index("sta")


class Places:
    def __init__(self, sizes):
        self.tm_count, self.sta_count = sizes[0], sizes[1]
        self.x_count = self.sta_count // 2
        self.me_t, self.me_s = position()
        self.offsets = [
            (dx, dy) for dx in range(self.x_count) for dy in range(2) if (dx, dy) != (0, 0)
        ]
        self.order = sorted(
            self.offsets, key=lambda o: -(min(o[0], self.x_count - o[0]) + 2 * o[1])
        ) + [(0, 0)]

    def time_device(self, by):
        return self.me_t + by

    def has(self, by):
        return self.me_t + by >= 0 if by < 0 else self.me_t + by < self.tm_count

    def station_device(self, dx, dy):
        x = lax.rem(self.me_s // 2 + dx, self.x_count)
        return 2 * x + lax.rem(lax.rem(self.me_s, 2) + dy, 2)


def greet(places):
    barrier = pltpu.get_barrier_semaphore()
    for by in (-2, -1, 1, 2):

        @pl.when(places.has(by))
        def _():
            pl.semaphore_signal(
                barrier, inc=1, device_id={"tm": places.time_device(by)}, device_id_type=MESH
            )

    for dx, dy in places.offsets:
        pl.semaphore_signal(
            barrier, inc=1, device_id={"sta": places.station_device(dx, dy)}, device_id_type=MESH
        )


def await_greetings(places):
    near = sum(jnp.where(places.has(by), 1, 0) for by in (-2, -1, 1, 2))
    pl.semaphore_wait(pltpu.get_barrier_semaphore(), near + len(places.offsets))


def halo_copies(places, slab, window, halo_send, halo_recv):
    def halo(slot, by, src, dst, width):
        copy = pltpu.make_async_remote_copy(
            src_ref=window.at[:, pl.ds(src, width)],
            dst_ref=window.at[:, pl.ds(dst, width)],
            send_sem=halo_send.at[slot],
            recv_sem=halo_recv.at[slot],
            device_id={"tm": places.time_device(by)},
            device_id_type=MESH,
        )
        return copy, by

    rest = (BLOCKS + 1) * LANE - (LANE + 2 * slab)
    return [
        halo(0, -2, LANE, LANE + 2 * slab, rest),
        halo(1, -1, LANE, LANE + slab, slab),
        halo(2, 1, slab, 0, LANE),
    ]


def start_halo(places, halos):
    for copy, by in halos:
        pl.when(places.has(by))(copy.start)


def await_halo(places, halos):
    for copy, by in halos:
        pl.when(places.has(-by))(copy.wait_recv)
    for copy, by in halos:
        pl.when(places.has(by))(copy.wait_send)


def prepare_template(values):
    values = values.astype(jnp.float32)
    mean = jnp.sum(values, axis=0, keepdims=True) * (1.0 / TLEN)
    centred = values - mean
    power = jnp.sum(centred * centred, axis=0, keepdims=True) * (1.0 / TLEN)
    factor = lax.rsqrt(power + 1e-06) * (1.0 / math.sqrt(TLEN))
    scaled = centred * factor
    return jnp.transpose(scaled).astype(jnp.bfloat16)


def store_in_order(places, share, rows, ref):
    order = [places.station_device(dx, dy) for dx, dy in places.order]
    for block in range(places.sta_count):
        slot = sum(jnp.where(peer == block, i, 0) for i, peer in enumerate(order))
        start = pl.multiple_of(slot * share, share)
        ref[pl.ds(start, share), :] = rows[share * block : share * (block + 1)]


def prepare_templates(places, share, raw_templates, unit):
    for c in range(unit.shape[0]):
        store_in_order(places, share, prepare_template(raw_templates[c]), unit.at[c])


def bandpass(places, slab, window, bands):
    first = jnp.where(places.me_t == 0, 0.0, window[:, 0:LANE])
    raw = [first] + [window[:, LANE * b : LANE * (b + 1)] for b in range(1, BLOCKS + 1)]
    lows = jnp.concatenate(raw[:BLOCKS], axis=0)
    highs = jnp.concatenate(raw[1:], axis=0)
    filtered = jnp.dot(
        jnp.concatenate([lows, highs], axis=1),
        bands,
        precision=lax.Precision.HIGHEST,
        preferred_element_type=jnp.float32,
    )
    remaining = (places.tm_count - places.me_t) * slab
    return [
        jnp.where(b * LANE < remaining, filtered[8 * b : 8 * b + 8], 0.0) for b in range(BLOCKS)
    ]


def window_norm(blocks, mask):
    series = jnp.concatenate(blocks, axis=1)
    level = jnp.concatenate([series, series * series], axis=0)
    kept = {}
    for bit in range(9):
        if bit in (4, 7, 8):
            kept[bit] = level
        if bit < 8:
            level = level + shifted_left(level, 1 << bit)
    sums = kept[8] + shifted_left(kept[7], 256) + shifted_left(kept[4], 384)
    window_sum, window_power = sums[0:8, : 8 * LANE], sums[8:16, : 8 * LANE]
    inverse_norm = lax.rsqrt(
        jnp.maximum(window_power - window_sum * window_sum * (1.0 / TLEN), 1.0)
    )
    row = lax.broadcasted_iota(jnp.int32, (8, 8 * LANE), 0)
    return inverse_norm * jnp.where(row < 3, mask[0], mask[1]).astype(jnp.float32)


def build_hankel(blocks, hankel):
    lane = lax.broadcasted_iota(jnp.int32, (LANE, LANE), 1)
    line = lax.broadcasted_iota(jnp.int32, (LANE, LANE), 0)
    inside = lane + line < LANE
    turn = lax.rem(lane + line, LANE)
    for c in range(hankel.shape[0]):
        turned = [
            jnp.take_along_axis(
                jnp.broadcast_to(blocks[b][c : c + 1], (LANE, LANE)),
                turn,
                axis=1,
                mode="promise_in_bounds",
            )
            for b in range(BLOCKS)
        ]
        turned.append(jnp.zeros((LANE, LANE), jnp.float32))
        for b in range(BLOCKS):
            hankel[c, :, LANE * b : LANE * (b + 1)] = jnp.where(
                inside, turned[b], turned[b + 1]
            ).astype(jnp.bfloat16)


def correlate(c, rows, unit, hankel):
    matrix = jnp.concatenate(
        [
            hankel[c, 0 : min(LANE, TLEN - LANE * m), LANE * m : LANE * (m + 8)]
            for m in range(4)
        ],
        axis=0,
    )
    return jnp.dot(rows, matrix, preferred_element_type=jnp.float32)


def moved(products, inverse_norm, delay):
    rows = products.shape[0]
    lane = lax.broadcasted_iota(jnp.int32, (rows, LANE), 1)
    by_256 = delay >= 256
    by_128 = lax.rem(delay, 256) >= 128
    fine = lax.rem(delay, 128)
    p = [
        products[:, LANE * b : LANE * (b + 1)] * inverse_norm[:, LANE * b : LANE * (b + 1)]
        for b in range(8)
    ]
    p = [jnp.where(by_256, p[b + 2], p[b]) for b in range(6)]
    p = [jnp.where(by_128, p[b + 1], p[b]) for b in range(5)]
    source = lax.rem(lane + fine, LANE)
    ahead = lane < fine
    return [
        jnp.take_along_axis(
            jnp.where(ahead, p[b + 1], p[b]), source, axis=1, mode="promise_in_bounds"
        )
        for b in range(4)
    ]


def match(first, count, delays, inverse_norm, unit, hankel, partial):
    total = None
    for c in range(unit.shape[0]):
        products = correlate(c, unit[c, first : first + count, :], unit, hankel)
        delay = jnp.broadcast_to(delays[first : first + count, c : c + 1], (count, LANE))
        terms = moved(products, inverse_norm[c : c + 1], delay)
        total = terms if total is None else [a + b for a, b in zip(total, terms)]
    for b in range(4):
        partial[first : first + count, LANE * b : LANE * (b + 1)] = total[b]


def send_sum(places, share, slot, partial, received, sum_send, sum_recv):
    copy = pltpu.make_async_remote_copy(
        src_ref=partial.at[pl.ds(share * slot, share)],
        dst_ref=received.at[slot],
        send_sem=sum_send.at[slot],
        recv_sem=sum_recv.at[slot],
        device_id={"sta": places.station_device(*places.order[slot])},
        device_id_type=MESH,
    )
    copy.start()
    return copy


def add_received(places, share, copies, partial, received, out_ref):
    result = partial[share * len(copies) :, :]
    for slot, copy in enumerate(copies):
        copy.wait()
        result = result + received[slot]
    out_ref[...] = result


def kernel(
    sizes,
    traces_ref,
    taps_ref,
    templates_ref,
    moveouts_ref,
    mask_ref,
    out_ref,
    samples,
    taps,
    moveouts,
    mask,
    window,
    raw_templates,
    unit,
    delays,
    hankel,
    partial,
    received,
    local_sem,
    halo_send,
    halo_recv,
    sum_send,
    sum_recv,
):
    slab, channels, share = sizes[2:]
    kcount = share * sizes[1]
    places = Places(sizes)
    fetches = [
        pltpu.make_async_copy(src, dst, local_sem.at[i])
        for i, (src, dst) in enumerate(
            [(traces_ref, samples), (taps_ref, taps), (moveouts_ref, moveouts), (mask_ref, mask)]
            + [(templates_ref.at[c], raw_templates.at[c]) for c in range(channels)]
        )
    ]
    for fetch in fetches:
        fetch.start()
    window[...] = jnp.zeros_like(window)
    greet(places)
    fetches[0].wait()
    window[0:channels, LANE : LANE + slab] = samples[...]
    await_greetings(places)
    halos = halo_copies(places, slab, window, halo_send, halo_recv)
    start_halo(places, halos)
    fetches[1].wait()
    bands = toeplitz(taps[...])
    fetches[2].wait()
    turned = jnp.transpose(
        jnp.concatenate([moveouts[...], jnp.zeros((8 - channels, kcount), jnp.int32)], axis=0)
    )
    store_in_order(places, share, turned, delays)
    for fetch in fetches[3:]:
        fetch.wait()
    prepare_templates(places, share, raw_templates, unit)
    await_halo(places, halos)
    blocks = bandpass(places, slab, window, bands)
    inverse_norm = window_norm(blocks, mask)
    build_hankel(blocks, hankel)
    copies = []
    first = 0
    for group in CHUNKS:
        match(first * share, group * share, delays, inverse_norm, unit, hankel, partial)
        for slot in range(first, min(first + group, places.sta_count - 1)):
            copies.append(send_sum(places, share, slot, partial, received, sum_send, sum_recv))
        first += group
    add_received(places, share, copies, partial, received, out_ref)


def per_device(sizes, traces, taps, templates, moveouts, mask):
    tm_count, sta_count, slab, channels, share = sizes
    kcount = share * sta_count
    vmem = pl.BlockSpec(memory_space=pltpu.VMEM)
    hbm = pl.BlockSpec(memory_space=pltpu.HBM)
    return pl.pallas_call(
        functools.partial(kernel, sizes),
        out_shape=jax.ShapeDtypeStruct((share, slab), jnp.float32),
        in_specs=[hbm] * 5,
        out_specs=vmem,
        scratch_shapes=[
            pltpu.VMEM((channels, slab), jnp.float32),
            pltpu.VMEM((1, LANE), jnp.float32),
            pltpu.VMEM((channels, kcount), jnp.int32),
            pltpu.SMEM((2,), jnp.int32),
            pltpu.VMEM((8, (BLOCKS + 1) * LANE), jnp.float32),
            pltpu.VMEM((channels, TLEN, kcount), jnp.bfloat16),
            pltpu.VMEM((channels, kcount, TLEN), jnp.bfloat16),
            pltpu.VMEM((kcount, 8), jnp.int32),
            pltpu.VMEM((channels, LANE, BLOCKS * LANE), jnp.bfloat16),
            pltpu.VMEM((kcount, slab), jnp.float32),
            pltpu.VMEM((sta_count - 1, share, slab), jnp.float32),
            pltpu.SemaphoreType.DMA((4 + channels,)),
            pltpu.SemaphoreType.DMA((3,)),
            pltpu.SemaphoreType.DMA((3,)),
            pltpu.SemaphoreType.DMA((sta_count - 1,)),
            pltpu.SemaphoreType.DMA((sta_count - 1,)),
        ],
        compiler_params=pltpu.CompilerParams(
            collective_id=0, has_side_effects=True, vmem_limit_bytes=24 * 2**20
        ),
        cost_estimate=pl.CostEstimate(
            flops=2 * kcount * channels * 512 * 1024, bytes_accessed=4 * 2**20, transcendentals=0
        ),
        name="network_match",
    )(
        *(
            pltpu.with_memory_space_constraint(array, pltpu.HBM)
            for array in (
                traces,
                taps.reshape(1, LANE),
                jnp.transpose(templates, (1, 2, 0)),
                jnp.transpose(moveouts),
                mask,
            )
        )
    )


def solution(mesh):
    tm_count, sta_count = mesh.shape["tm"], mesh.shape["sta"]

    def run(traces, taps, templates, moveouts, mask):
        sizes = (
            tm_count,
            sta_count,
            traces.shape[1] // tm_count,
            traces.shape[0] // sta_count,
            templates.shape[0] // sta_count,
        )
        return jax.shard_map(
            functools.partial(per_device, sizes),
            mesh=mesh,
            in_specs=(P("sta", "tm"), P(), P(None, "sta", None), P(None, "sta"), P("sta")),
            out_specs=P("sta", "tm"),
            check_vma=False,
        )(traces, taps, templates, moveouts, mask)

    return run
```

```python
import functools
import math

import jax
import jax.numpy as jnp
from jax import lax
from jax.experimental import pallas as pl
from jax.experimental.pallas import tpu as pltpu
from jax.sharding import PartitionSpec as P

TLEN = 400
DMAX = 400
LANE = 128
BLOCKS = 11
CHUNKS = (4, 4)
MESH = pl.DeviceIdType.MESH


def shifted_left(values, step):
    extent = values.shape[-1]
    if step % LANE == 0:
        return jnp.concatenate([values[:, step:], values[:, :step]], axis=1)
    return pltpu.roll(values, extent - step, 1)


def toeplitz(taps):
    rows = jnp.broadcast_to(taps, (LANE, LANE))
    turned = pltpu.roll(rows, 0, 1, stride=1, stride_axis=0)
    row = lax.broadcasted_iota(jnp.int32, (LANE, LANE), 0)
    lane = lax.broadcasted_iota(jnp.int32, (LANE, LANE), 1)
    below = jnp.where(lane >= row, turned, 0.0)
    above = jnp.where(lane < row, turned, 0.0)
    return jnp.concatenate([above, below], axis=0)


def position():
    return lax.axis_index("tm"), lax.axis_index("sta")


class Places:
    def __init__(self, sizes):
        self.tm_count, self.sta_count = sizes[0], sizes[1]
        self.x_count = self.sta_count // 2
        self.me_t, self.me_s = position()
        self.offsets = [
            (dx, dy) for dx in range(self.x_count) for dy in range(2) if (dx, dy) != (0, 0)
        ]
        self.order = sorted(
            self.offsets, key=lambda o: -(min(o[0], self.x_count - o[0]) + 2 * o[1])
        ) + [(0, 0)]

    def time_device(self, by):
        return self.me_t + by

    def has(self, by):
        return self.me_t + by >= 0 if by < 0 else self.me_t + by < self.tm_count

    def station_device(self, dx, dy):
        x = lax.rem(self.me_s // 2 + dx, self.x_count)
        return 2 * x + lax.rem(lax.rem(self.me_s, 2) + dy, 2)


def greet(places):
    barrier = pltpu.get_barrier_semaphore()
    for by in (-2, -1, 1, 2):

        @pl.when(places.has(by))
        def _():
            pl.semaphore_signal(
                barrier, inc=1, device_id={"tm": places.time_device(by)}, device_id_type=MESH
            )

    for dx, dy in places.offsets:
        pl.semaphore_signal(
            barrier, inc=1, device_id={"sta": places.station_device(dx, dy)}, device_id_type=MESH
        )


def await_greetings(places):
    near = sum(jnp.where(places.has(by), 1, 0) for by in (-2, -1, 1, 2))
    pl.semaphore_wait(pltpu.get_barrier_semaphore(), near + len(places.offsets))


def halo_copies(places, slab, window, halo_send, halo_recv):
    def halo(slot, by, src, dst, width):
        copy = pltpu.make_async_remote_copy(
            src_ref=window.at[:, pl.ds(src, width)],
            dst_ref=window.at[:, pl.ds(dst, width)],
            send_sem=halo_send.at[slot],
            recv_sem=halo_recv.at[slot],
            device_id={"tm": places.time_device(by)},
            device_id_type=MESH,
        )
        return copy, by

    rest = (BLOCKS + 1) * LANE - (LANE + 2 * slab)
    return [
        halo(0, -2, LANE, LANE + 2 * slab, rest),
        halo(1, -1, LANE, LANE + slab, slab),
        halo(2, 1, slab, 0, LANE),
    ]


def start_halo(places, halos):
    for copy, by in halos:
        pl.when(places.has(by))(copy.start)


def await_halo(places, halos):
    for copy, by in halos:
        pl.when(places.has(-by))(copy.wait_recv)


def finish_halo(places, halos):
    for copy, by in halos:
        pl.when(places.has(by))(copy.wait_send)


def prepare_template(values):
    values = values.astype(jnp.float32)
    mean = jnp.sum(values, axis=0, keepdims=True) * (1.0 / TLEN)
    centred = values - mean
    power = jnp.sum(centred * centred, axis=0, keepdims=True) * (1.0 / TLEN)
    factor = lax.rsqrt(power + 1e-06) * (1.0 / math.sqrt(TLEN))
    scaled = centred * factor
    groups = scaled.reshape(TLEN // 8, 8, values.shape[1])
    back = 7 - lax.broadcasted_iota(jnp.int32, groups.shape, 1)
    reversed_groups = jnp.take_along_axis(groups, back, axis=1, mode="promise_in_bounds")
    return jnp.transpose(reversed_groups.reshape(scaled.shape)).astype(jnp.bfloat16)


def store_in_order(places, share, rows, ref):
    order = [places.station_device(dx, dy) for dx, dy in places.order]
    for block in range(places.sta_count):
        slot = sum(jnp.where(peer == block, i, 0) for i, peer in enumerate(order))
        start = pl.multiple_of(slot * share, share)
        ref[pl.ds(start, share), :] = rows[share * block : share * (block + 1)]


def prepare_templates(places, share, raw_templates, unit):
    for c in range(unit.shape[0]):
        store_in_order(places, share, prepare_template(raw_templates[c]), unit.at[c])


def bandpass(places, slab, window, bands):
    first = jnp.where(places.me_t == 0, 0.0, window[:, 0:LANE])
    raw = [first] + [window[:, LANE * b : LANE * (b + 1)] for b in range(1, BLOCKS + 1)]
    lows = jnp.concatenate(raw[:BLOCKS], axis=0)
    highs = jnp.concatenate(raw[1:], axis=0)
    filtered = jnp.dot(
        jnp.concatenate([lows, highs], axis=1),
        bands,
        precision=lax.Precision.HIGHEST,
        preferred_element_type=jnp.float32,
    )
    remaining = (places.tm_count - places.me_t) * slab
    return [
        jnp.where(b * LANE < remaining, filtered[8 * b : 8 * b + 8], 0.0) for b in range(BLOCKS)
    ]


def window_bands():
    row = lax.broadcasted_iota(jnp.int32, (5 * LANE, LANE), 0)
    lane = lax.broadcasted_iota(jnp.int32, (5 * LANE, LANE), 1)
    ahead = row - lane
    return jnp.where((ahead >= 0) & (ahead < TLEN), 1.0, 0.0).astype(jnp.bfloat16)


def window_norm(blocks, mask):
    padded = blocks + [jnp.zeros((8, LANE), jnp.float32)]
    both = [jnp.concatenate([block, block * block], axis=0) for block in padded]
    pieces = []
    for _ in range(3):
        rounded = [block.astype(jnp.bfloat16) for block in both]
        both = [block - part.astype(jnp.float32) for block, part in zip(both, rounded)]
        pieces += [jnp.concatenate(rounded[b : b + 5], axis=1) for b in range(8)]
    sums = jnp.dot(
        jnp.concatenate(pieces, axis=0), window_bands(), preferred_element_type=jnp.float32
    )
    sums = (sums[256:384] + sums[128:256]) + sums[0:128]
    window_sum = jnp.concatenate([sums[16 * b : 16 * b + 8] for b in range(8)], axis=1)
    window_power = jnp.concatenate([sums[16 * b + 8 : 16 * b + 16] for b in range(8)], axis=1)
    inverse_norm = lax.rsqrt(
        jnp.maximum(window_power - window_sum * window_sum * (1.0 / TLEN), 1.0)
    )
    row = lax.broadcasted_iota(jnp.int32, (8, 8 * LANE), 0)
    return inverse_norm * jnp.where(row < 3, mask[0], mask[1]).astype(jnp.float32)


def build_hankel(blocks, hankel):
    lane = lax.broadcasted_iota(jnp.int32, (8, LANE), 1)
    line = lax.broadcasted_iota(jnp.int32, (8, LANE), 0)
    for c in range(hankel.shape[0]):
        rows = [jnp.broadcast_to(blocks[b][c : c + 1], (8, LANE)) for b in range(BLOCKS)]
        for g in range(0, 16, 2):
            halves = []
            for h in (g, g + 1):
                turned = [pltpu.roll(row, 121 - 8 * h, 1, stride=1, stride_axis=0) for row in rows]
                turned.append(jnp.zeros((8, LANE), jnp.float32))
                inside = lane + (8 * h + 7) - line < LANE
                halves.append(
                    [jnp.where(inside, turned[b], turned[b + 1]) for b in range(BLOCKS)]
                )
            for b in range(BLOCKS):
                hankel[c, 8 * g : 8 * g + 16, LANE * b : LANE * (b + 1)] = jnp.concatenate(
                    [halves[0][b], halves[1][b]], axis=0
                ).astype(jnp.bfloat16)


def correlate(c, rows, unit, hankel):
    matrix = jnp.concatenate(
        [
            hankel[c, 0 : min(LANE, TLEN - LANE * m), LANE * m : LANE * (m + 8)]
            for m in range(4)
        ],
        axis=0,
    )
    return jnp.dot(rows, matrix, preferred_element_type=jnp.float32)


def moved(products, inverse_norm, delay):
    rows = products.shape[0]
    lane = lax.broadcasted_iota(jnp.int32, (rows, LANE), 1)
    by_256 = delay >= 256
    by_128 = lax.rem(delay, 256) >= 128
    fine = lax.rem(delay, 128)
    p = [
        products[:, LANE * b : LANE * (b + 1)] * inverse_norm[:, LANE * b : LANE * (b + 1)]
        for b in range(8)
    ]
    p = [jnp.where(by_256, p[b + 2], p[b]) for b in range(6)]
    p = [jnp.where(by_128, p[b + 1], p[b]) for b in range(5)]
    source = lax.rem(lane + fine, LANE)
    ahead = lane < fine
    return [
        jnp.take_along_axis(
            jnp.where(ahead, p[b + 1], p[b]), source, axis=1, mode="promise_in_bounds"
        )
        for b in range(4)
    ]


def match(first, count, delays, inverse_norm, unit, hankel, partial):
    total = None
    for c in range(unit.shape[0]):
        products = correlate(c, unit[c, first : first + count, :], unit, hankel)
        delay = jnp.broadcast_to(delays[first : first + count, c : c + 1], (count, LANE))
        terms = moved(products, inverse_norm[c : c + 1], delay)
        total = terms if total is None else [a + b for a, b in zip(total, terms)]
    for b in range(4):
        partial[first : first + count, LANE * b : LANE * (b + 1)] = total[b]


def send_sum(places, share, slot, partial, received, sum_send, sum_recv):
    copy = pltpu.make_async_remote_copy(
        src_ref=partial.at[pl.ds(share * slot, share)],
        dst_ref=received.at[slot],
        send_sem=sum_send.at[slot],
        recv_sem=sum_recv.at[slot],
        device_id={"sta": places.station_device(*places.order[slot])},
        device_id_type=MESH,
    )
    copy.start()
    return copy


def add_received(places, share, copies, partial, received, out_ref):
    result = partial[share * len(copies) :, :]
    for slot, copy in enumerate(copies):
        copy.wait_recv()
        result = result + received[slot]
    out_ref[...] = result
    for copy in copies:
        copy.wait_send()


def kernel(
    sizes,
    traces_ref,
    taps_ref,
    templates_ref,
    moveouts_ref,
    mask_ref,
    out_ref,
    samples,
    taps,
    moveouts,
    mask,
    window,
    raw_templates,
    unit,
    delays,
    hankel,
    partial,
    received,
    local_sem,
    halo_send,
    halo_recv,
    sum_send,
    sum_recv,
):
    slab, channels, share = sizes[2:]
    kcount = share * sizes[1]
    places = Places(sizes)
    fetches = [
        pltpu.make_async_copy(src, dst, local_sem.at[i])
        for i, (src, dst) in enumerate(
            [(traces_ref, samples), (taps_ref, taps), (moveouts_ref, moveouts), (mask_ref, mask)]
            + [(templates_ref.at[c], raw_templates.at[c]) for c in range(channels)]
        )
    ]
    for fetch in fetches:
        fetch.start()
    window[...] = jnp.zeros_like(window)
    greet(places)
    fetches[0].wait()
    window[0:channels, LANE : LANE + slab] = samples[...]
    await_greetings(places)
    halos = halo_copies(places, slab, window, halo_send, halo_recv)
    start_halo(places, halos)
    fetches[1].wait()
    bands = toeplitz(taps[...])
    fetches[2].wait()
    turned = jnp.transpose(
        jnp.concatenate([moveouts[...], jnp.zeros((8 - channels, kcount), jnp.int32)], axis=0)
    )
    store_in_order(places, share, turned, delays)
    for fetch in fetches[3:]:
        fetch.wait()
    prepare_templates(places, share, raw_templates, unit)
    await_halo(places, halos)
    blocks = bandpass(places, slab, window, bands)
    inverse_norm = window_norm(blocks, mask)
    build_hankel(blocks, hankel)
    copies = []
    first = 0
    for group in CHUNKS:
        match(first * share, group * share, delays, inverse_norm, unit, hankel, partial)
        for slot in range(first, min(first + group, places.sta_count - 1)):
            copies.append(send_sum(places, share, slot, partial, received, sum_send, sum_recv))
        first += group
    add_received(places, share, copies, partial, received, out_ref)
    finish_halo(places, halos)


def per_device(sizes, traces, taps, templates, moveouts, mask):
    tm_count, sta_count, slab, channels, share = sizes
    kcount = share * sta_count
    vmem = pl.BlockSpec(memory_space=pltpu.VMEM)
    hbm = pl.BlockSpec(memory_space=pltpu.HBM)
    return pl.pallas_call(
        functools.partial(kernel, sizes),
        out_shape=jax.ShapeDtypeStruct((share, slab), jnp.float32),
        in_specs=[hbm] * 5,
        out_specs=vmem,
        scratch_shapes=[
            pltpu.VMEM((channels, slab), jnp.float32),
            pltpu.VMEM((1, LANE), jnp.float32),
            pltpu.VMEM((channels, kcount), jnp.int32),
            pltpu.SMEM((2,), jnp.int32),
            pltpu.VMEM((8, (BLOCKS + 1) * LANE), jnp.float32),
            pltpu.VMEM((channels, TLEN, kcount), jnp.bfloat16),
            pltpu.VMEM((channels, kcount, TLEN), jnp.bfloat16),
            pltpu.VMEM((kcount, 8), jnp.int32),
            pltpu.VMEM((channels, LANE, BLOCKS * LANE), jnp.bfloat16),
            pltpu.VMEM((kcount, slab), jnp.float32),
            pltpu.VMEM((sta_count - 1, share, slab), jnp.float32),
            pltpu.SemaphoreType.DMA((4 + channels,)),
            pltpu.SemaphoreType.DMA((3,)),
            pltpu.SemaphoreType.DMA((3,)),
            pltpu.SemaphoreType.DMA((sta_count - 1,)),
            pltpu.SemaphoreType.DMA((sta_count - 1,)),
        ],
        compiler_params=pltpu.CompilerParams(
            collective_id=0, has_side_effects=True, vmem_limit_bytes=24 * 2**20
        ),
        cost_estimate=pl.CostEstimate(
            flops=2 * kcount * channels * 512 * 1024, bytes_accessed=4 * 2**20, transcendentals=0
        ),
        name="network_match",
    )(
        *(
            pltpu.with_memory_space_constraint(array, pltpu.HBM)
            for array in (
                traces,
                taps.reshape(1, LANE),
                jnp.transpose(templates, (1, 2, 0)),
                jnp.transpose(moveouts),
                mask,
            )
        )
    )


def solution(mesh):
    tm_count, sta_count = mesh.shape["tm"], mesh.shape["sta"]

    def run(traces, taps, templates, moveouts, mask):
        sizes = (
            tm_count,
            sta_count,
            traces.shape[1] // tm_count,
            traces.shape[0] // sta_count,
            templates.shape[0] // sta_count,
        )
        return jax.shard_map(
            functools.partial(per_device, sizes),
            mesh=mesh,
            in_specs=(P("sta", "tm"), P(), P(None, "sta", None), P(None, "sta"), P("sta")),
            out_specs=P("sta", "tm"),
            check_vma=False,
        )(traces, taps, templates, moveouts, mask)

    return run
```

```python
import functools
import math

import jax
import jax.numpy as jnp
from jax import lax
from jax.experimental import pallas as pl
from jax.experimental.pallas import tpu as pltpu
from jax.sharding import PartitionSpec as P

TLEN = 400
DMAX = 400
LANE = 128
BLOCKS = 11
CHUNKS = (4, 4)
MESH = pl.DeviceIdType.MESH


def shifted_left(values, step):
    extent = values.shape[-1]
    if step % LANE == 0:
        return jnp.concatenate([values[:, step:], values[:, :step]], axis=1)
    return pltpu.roll(values, extent - step, 1)


def toeplitz(taps):
    rows = jnp.broadcast_to(taps, (LANE, LANE))
    turned = pltpu.roll(rows, 0, 1, stride=1, stride_axis=0)
    row = lax.broadcasted_iota(jnp.int32, (LANE, LANE), 0)
    lane = lax.broadcasted_iota(jnp.int32, (LANE, LANE), 1)
    below = jnp.where(lane >= row, turned, 0.0)
    above = jnp.where(lane < row, turned, 0.0)
    return jnp.concatenate([above, below], axis=0)


def position():
    return lax.axis_index("tm"), lax.axis_index("sta")


class Places:
    def __init__(self, sizes):
        self.tm_count, self.sta_count = sizes[0], sizes[1]
        self.x_count = self.sta_count // 2
        self.me_t, self.me_s = position()
        self.offsets = [
            (dx, dy) for dx in range(self.x_count) for dy in range(2) if (dx, dy) != (0, 0)
        ]
        x, y = lax.shift_right_logical(self.me_s, 1), self.me_s & 1
        at_start = self.me_t == 0

        def turn(x, y):
            first = at_start & (x + y == 0)
            return jnp.where(first, self.sta_count, y * self.x_count + x)

        mine = turn(x, y)
        self.peers, self.later = {(0, 0): self.me_s}, {}
        for dx, dy in self.offsets:
            peer_x, peer_y = (x + dx) & (self.x_count - 1), y ^ dy
            self.peers[dx, dy] = 2 * peer_x + peer_y
            self.later[dx, dy] = turn(peer_x, peer_y) < mine
        self.order = sorted(
            self.offsets, key=lambda o: -(min(o[0], self.x_count - o[0]) + 2 * o[1])
        ) + [(0, 0)]

    def time_device(self, by):
        return self.me_t + by

    def has(self, by):
        return self.me_t + by >= 0 if by < 0 else self.me_t + by < self.tm_count

    def last_to_come(self, by):
        if by > 0:
            return self.me_t == 0
        return self.me_t + by != 0

    def later_peer(self, dx, dy):
        return self.later[dx, dy]

    def station_device(self, dx, dy):
        return self.peers[dx, dy]


def greet(places):
    barrier = pltpu.get_barrier_semaphore()
    for by in (-2, -1, 1, 2):

        @pl.when(places.has(by) & jnp.logical_not(places.last_to_come(by)))
        def _():
            pl.semaphore_signal(
                barrier, inc=1, device_id={"tm": places.time_device(by)}, device_id_type=MESH
            )

    for dx, dy in places.offsets:

        @pl.when(jnp.logical_not(places.later_peer(dx, dy)))
        def _():
            pl.semaphore_signal(
                barrier,
                inc=1,
                device_id={"sta": places.station_device(dx, dy)},
                device_id_type=MESH,
            )


def await_greetings(places):
    near = sum(
        jnp.where(places.has(by) & places.last_to_come(by), 1, 0) for by in (-2, -1, 1, 2)
    )
    far = sum(jnp.where(places.later_peer(dx, dy), 1, 0) for dx, dy in places.offsets)
    barrier = pltpu.get_barrier_semaphore()

    @pl.when(near + far > 0)
    def _():
        pl.semaphore_wait(barrier, near + far)


def answer_near(places, near_sem):
    for by in (-1, 1, 2):

        @pl.when(places.has(by) & places.last_to_come(by))
        def _():
            pl.semaphore_signal(
                near_sem.at[2 - by],
                inc=1,
                device_id={"tm": places.time_device(by)},
                device_id_type=MESH,
            )


def answer_far(places, far_sem):
    for dx, dy in places.offsets:
        back = (-dx % places.x_count, dy)

        @pl.when(places.later_peer(dx, dy))
        def _():
            pl.semaphore_signal(
                far_sem.at[places.offsets.index(back)],
                inc=1,
                device_id={"sta": places.station_device(dx, dy)},
                device_id_type=MESH,
            )


def halo_copies(places, slab, window, halo_send, halo_recv):
    def halo(slot, by, src, dst, width):
        copy = pltpu.make_async_remote_copy(
            src_ref=window.at[:, pl.ds(src, width)],
            dst_ref=window.at[:, pl.ds(dst, width)],
            send_sem=halo_send.at[slot],
            recv_sem=halo_recv.at[slot],
            device_id={"tm": places.time_device(by)},
            device_id_type=MESH,
        )
        return copy, by

    rest = (BLOCKS + 1) * LANE - (LANE + 2 * slab)
    return [
        halo(0, -2, LANE, LANE + 2 * slab, rest),
        halo(1, -1, LANE, LANE + slab, slab),
        halo(2, 1, slab, 0, LANE),
    ]


def start_halo(places, halos, near_sem):
    for copy, by in halos:
        pl.when(places.has(by) & places.last_to_come(by))(copy.start)
    answer_near(places, near_sem)
    for copy, by in halos:

        @pl.when(places.has(by) & jnp.logical_not(places.last_to_come(by)))
        def _():
            pl.semaphore_wait(near_sem.at[2 + by], 1)
            copy.start()


def await_halo(places, halos):
    for copy, by in halos:
        pl.when(places.has(-by))(copy.wait_recv)


def finish_halo(places, halos):
    for copy, by in halos:
        pl.when(places.has(by))(copy.wait_send)


def prepare_template(values):
    values = values.astype(jnp.float32)
    mean = jnp.sum(values, axis=0, keepdims=True) * (1.0 / TLEN)
    centred = values - mean
    power = jnp.sum(centred * centred, axis=0, keepdims=True) * (1.0 / TLEN)
    factor = lax.rsqrt(power + 1e-06) * (1.0 / math.sqrt(TLEN))
    scaled = centred * factor
    groups = scaled.reshape(TLEN // 8, 8, values.shape[1])
    back = 7 - lax.broadcasted_iota(jnp.int32, groups.shape, 1)
    reversed_groups = jnp.take_along_axis(groups, back, axis=1, mode="promise_in_bounds")
    return jnp.transpose(reversed_groups.reshape(scaled.shape)).astype(jnp.bfloat16)


def store_in_order(places, share, rows, ref):
    order = [places.station_device(dx, dy) for dx, dy in places.order]
    for block in range(places.sta_count):
        slot = sum(jnp.where(peer == block, i, 0) for i, peer in enumerate(order))
        start = pl.multiple_of(slot * share, share)
        ref[pl.ds(start, share), :] = rows[share * block : share * (block + 1)]


def prepare_templates(places, share, raw_templates, unit):
    for c in range(unit.shape[0]):
        store_in_order(places, share, prepare_template(raw_templates[c]), unit.at[c])


def bandpass(places, slab, window, bands):
    first = jnp.where(places.me_t == 0, 0.0, window[:, 0:LANE])
    raw = [first] + [window[:, LANE * b : LANE * (b + 1)] for b in range(1, BLOCKS + 1)]
    lows = jnp.concatenate(raw[:BLOCKS], axis=0)
    highs = jnp.concatenate(raw[1:], axis=0)
    filtered = jnp.dot(
        jnp.concatenate([lows, highs], axis=1),
        bands,
        precision=lax.Precision.HIGHEST,
        preferred_element_type=jnp.float32,
    )
    remaining = (places.tm_count - places.me_t) * slab
    return [
        jnp.where(b * LANE < remaining, filtered[8 * b : 8 * b + 8], 0.0) for b in range(BLOCKS)
    ]


def window_bands():
    row = lax.broadcasted_iota(jnp.int32, (5 * LANE, LANE), 0)
    lane = lax.broadcasted_iota(jnp.int32, (5 * LANE, LANE), 1)
    ahead = row - lane
    return jnp.where((ahead >= 0) & (ahead < TLEN), 1.0, 0.0).astype(jnp.bfloat16)


def window_norm(blocks, mask):
    padded = blocks + [jnp.zeros((8, LANE), jnp.float32)]
    both = [jnp.concatenate([block, block * block], axis=0) for block in padded]
    pieces = []
    for _ in range(3):
        rounded = [block.astype(jnp.bfloat16) for block in both]
        both = [block - part.astype(jnp.float32) for block, part in zip(both, rounded)]
        pieces += [jnp.concatenate(rounded[b : b + 5], axis=1) for b in range(8)]
    sums = jnp.dot(
        jnp.concatenate(pieces, axis=0), window_bands(), preferred_element_type=jnp.float32
    )
    sums = (sums[256:384] + sums[128:256]) + sums[0:128]
    window_sum = jnp.concatenate([sums[16 * b : 16 * b + 8] for b in range(8)], axis=1)
    window_power = jnp.concatenate([sums[16 * b + 8 : 16 * b + 16] for b in range(8)], axis=1)
    inverse_norm = lax.rsqrt(
        jnp.maximum(window_power - window_sum * window_sum * (1.0 / TLEN), 1.0)
    )
    row = lax.broadcasted_iota(jnp.int32, (8, 8 * LANE), 0)
    return inverse_norm * jnp.where(row < 3, mask[0], mask[1]).astype(jnp.float32)


def build_hankel(blocks, hankel):
    lane = lax.broadcasted_iota(jnp.int32, (8, LANE), 1)
    line = lax.broadcasted_iota(jnp.int32, (8, LANE), 0)
    for c in range(hankel.shape[0]):
        rows = [jnp.broadcast_to(blocks[b][c : c + 1], (8, LANE)) for b in range(BLOCKS)]
        for g in range(0, 16, 2):
            halves = []
            for h in (g, g + 1):
                turned = [pltpu.roll(row, 121 - 8 * h, 1, stride=1, stride_axis=0) for row in rows]
                turned.append(jnp.zeros((8, LANE), jnp.float32))
                inside = lane + (8 * h + 7) - line < LANE
                halves.append(
                    [jnp.where(inside, turned[b], turned[b + 1]) for b in range(BLOCKS)]
                )
            for b in range(BLOCKS):
                hankel[c, 8 * g : 8 * g + 16, LANE * b : LANE * (b + 1)] = jnp.concatenate(
                    [halves[0][b], halves[1][b]], axis=0
                ).astype(jnp.bfloat16)


def correlate(c, rows, unit, hankel):
    matrix = jnp.concatenate(
        [
            hankel[c, 0 : min(LANE, TLEN - LANE * m), LANE * m : LANE * (m + 8)]
            for m in range(4)
        ],
        axis=0,
    )
    return jnp.dot(rows, matrix, preferred_element_type=jnp.float32)


def moved(products, inverse_norm, delay):
    rows = products.shape[0]
    lane = lax.broadcasted_iota(jnp.int32, (rows, LANE), 1)
    by_256 = delay >= 256
    by_128 = lax.rem(delay, 256) >= 128
    fine = lax.rem(delay, 128)
    p = [
        products[:, LANE * b : LANE * (b + 1)] * inverse_norm[:, LANE * b : LANE * (b + 1)]
        for b in range(8)
    ]
    p = [jnp.where(by_256, p[b + 2], p[b]) for b in range(6)]
    p = [jnp.where(by_128, p[b + 1], p[b]) for b in range(5)]
    source = lax.rem(lane + fine, LANE)
    ahead = lane < fine
    return [
        jnp.take_along_axis(
            jnp.where(ahead, p[b + 1], p[b]), source, axis=1, mode="promise_in_bounds"
        )
        for b in range(4)
    ]


def match(first, count, delays, inverse_norm, unit, hankel, partial):
    total = None
    for c in range(unit.shape[0]):
        products = correlate(c, unit[c, first : first + count, :], unit, hankel)
        delay = jnp.broadcast_to(delays[first : first + count, c : c + 1], (count, LANE))
        terms = moved(products, inverse_norm[c : c + 1], delay)
        total = terms if total is None else [a + b for a, b in zip(total, terms)]
    for b in range(4):
        partial[first : first + count, LANE * b : LANE * (b + 1)] = total[b]


def send_sum(places, share, slot, partial, received, far_sem, sum_send, sum_recv):
    offset = places.order[slot]

    @pl.when(jnp.logical_not(places.later_peer(*offset)))
    def _():
        pl.semaphore_wait(far_sem.at[places.offsets.index(offset)], 1)

    copy = pltpu.make_async_remote_copy(
        src_ref=partial.at[pl.ds(share * slot, share)],
        dst_ref=received.at[slot],
        send_sem=sum_send.at[slot],
        recv_sem=sum_recv.at[slot],
        device_id={"sta": places.station_device(*offset)},
        device_id_type=MESH,
    )
    copy.start()
    return copy


def add_received(places, share, copies, partial, received, out_ref):
    result = partial[share * len(copies) :, :]
    for slot, copy in enumerate(copies):
        copy.wait_recv()
        result = result + received[slot]
    out_ref[...] = result
    for copy in copies:
        copy.wait_send()


def kernel(
    sizes,
    traces_ref,
    taps_ref,
    templates_ref,
    moveouts_ref,
    mask_ref,
    out_ref,
    samples,
    taps,
    moveouts,
    mask,
    window,
    raw_templates,
    unit,
    delays,
    hankel,
    partial,
    received,
    near_sem,
    far_sem,
    local_sem,
    halo_send,
    halo_recv,
    sum_send,
    sum_recv,
):
    slab, channels, share = sizes[2:]
    kcount = share * sizes[1]
    places = Places(sizes)
    fetches = [
        pltpu.make_async_copy(src, dst, local_sem.at[i])
        for i, (src, dst) in enumerate(
            [(traces_ref, samples), (taps_ref, taps), (moveouts_ref, moveouts), (mask_ref, mask)]
            + [(templates_ref.at[c], raw_templates.at[c]) for c in range(channels)]
        )
    ]
    for fetch in fetches:
        fetch.start()
    window[...] = jnp.zeros_like(window)
    greet(places)
    fetches[0].wait()
    window[0:channels, LANE : LANE + slab] = samples[...]
    await_greetings(places)
    halos = halo_copies(places, slab, window, halo_send, halo_recv)
    start_halo(places, halos, near_sem)
    answer_far(places, far_sem)
    fetches[1].wait()
    bands = toeplitz(taps[...])
    fetches[2].wait()
    turned = jnp.transpose(
        jnp.concatenate([moveouts[...], jnp.zeros((8 - channels, kcount), jnp.int32)], axis=0)
    )
    store_in_order(places, share, turned, delays)
    for fetch in fetches[3:]:
        fetch.wait()
    prepare_templates(places, share, raw_templates, unit)
    await_halo(places, halos)
    blocks = bandpass(places, slab, window, bands)
    inverse_norm = window_norm(blocks, mask)
    build_hankel(blocks, hankel)
    copies = []
    first = 0
    for group in CHUNKS:
        match(first * share, group * share, delays, inverse_norm, unit, hankel, partial)
        for slot in range(first, min(first + group, places.sta_count - 1)):
            copies.append(
                send_sum(places, share, slot, partial, received, far_sem, sum_send, sum_recv)
            )
        first += group
    add_received(places, share, copies, partial, received, out_ref)
    finish_halo(places, halos)


def per_device(sizes, traces, taps, templates, moveouts, mask):
    tm_count, sta_count, slab, channels, share = sizes
    kcount = share * sta_count
    vmem = pl.BlockSpec(memory_space=pltpu.VMEM)
    hbm = pl.BlockSpec(memory_space=pltpu.HBM)
    return pl.pallas_call(
        functools.partial(kernel, sizes),
        out_shape=jax.ShapeDtypeStruct((share, slab), jnp.float32),
        in_specs=[hbm] * 5,
        out_specs=vmem,
        scratch_shapes=[
            pltpu.VMEM((channels, slab), jnp.float32),
            pltpu.VMEM((1, LANE), jnp.float32),
            pltpu.VMEM((channels, kcount), jnp.int32),
            pltpu.SMEM((2,), jnp.int32),
            pltpu.VMEM((8, (BLOCKS + 1) * LANE), jnp.float32),
            pltpu.VMEM((channels, TLEN, kcount), jnp.bfloat16),
            pltpu.VMEM((channels, kcount, TLEN), jnp.bfloat16),
            pltpu.VMEM((kcount, 8), jnp.int32),
            pltpu.VMEM((channels, LANE, BLOCKS * LANE), jnp.bfloat16),
            pltpu.VMEM((kcount, slab), jnp.float32),
            pltpu.VMEM((sta_count - 1, share, slab), jnp.float32),
            pltpu.SemaphoreType.REGULAR((5,)),
            pltpu.SemaphoreType.REGULAR((sta_count - 1,)),
            pltpu.SemaphoreType.DMA((4 + channels,)),
            pltpu.SemaphoreType.DMA((3,)),
            pltpu.SemaphoreType.DMA((3,)),
            pltpu.SemaphoreType.DMA((sta_count - 1,)),
            pltpu.SemaphoreType.DMA((sta_count - 1,)),
        ],
        compiler_params=pltpu.CompilerParams(
            collective_id=0, has_side_effects=True, vmem_limit_bytes=24 * 2**20
        ),
        cost_estimate=pl.CostEstimate(
            flops=2 * kcount * channels * 512 * 1024, bytes_accessed=4 * 2**20, transcendentals=0
        ),
        name="network_match",
    )(
        *(
            pltpu.with_memory_space_constraint(array, pltpu.HBM)
            for array in (
                traces,
                taps.reshape(1, LANE),
                jnp.transpose(templates, (1, 2, 0)),
                jnp.transpose(moveouts),
                mask,
            )
        )
    )


def solution(mesh):
    tm_count, sta_count = mesh.shape["tm"], mesh.shape["sta"]

    def run(traces, taps, templates, moveouts, mask):
        sizes = (
            tm_count,
            sta_count,
            traces.shape[1] // tm_count,
            traces.shape[0] // sta_count,
            templates.shape[0] // sta_count,
        )
        return jax.shard_map(
            functools.partial(per_device, sizes),
            mesh=mesh,
            in_specs=(P("sta", "tm"), P(), P(None, "sta", None), P(None, "sta"), P("sta")),
            out_specs=P("sta", "tm"),
            check_vma=False,
        )(traces, taps, templates, moveouts, mask)

    return run
```

```python
import functools
import math

import jax
import jax.numpy as jnp
from jax import lax
from jax.experimental import pallas as pl
from jax.experimental.pallas import tpu as pltpu
from jax.sharding import PartitionSpec as P

TLEN = 400
DMAX = 400
LANE = 128
BLOCKS = 11
CHUNKS = (4, 4)
MESH = pl.DeviceIdType.MESH


def shifted_left(values, step):
    extent = values.shape[-1]
    if step % LANE == 0:
        return jnp.concatenate([values[:, step:], values[:, :step]], axis=1)
    return pltpu.roll(values, extent - step, 1)


def toeplitz(taps):
    rows = jnp.broadcast_to(taps, (LANE, LANE))
    turned = pltpu.roll(rows, 0, 1, stride=1, stride_axis=0)
    row = lax.broadcasted_iota(jnp.int32, (LANE, LANE), 0)
    lane = lax.broadcasted_iota(jnp.int32, (LANE, LANE), 1)
    below = jnp.where(lane >= row, turned, 0.0)
    above = jnp.where(lane < row, turned, 0.0)
    return jnp.concatenate([above, below], axis=0)


def position():
    return lax.axis_index("tm"), lax.axis_index("sta")


class Places:
    def __init__(self, sizes):
        self.tm_count, self.sta_count = sizes[0], sizes[1]
        self.x_count = self.sta_count // 2
        self.me_t, self.me_s = position()
        self.offsets = [
            (dx, dy) for dx in range(self.x_count) for dy in range(2) if (dx, dy) != (0, 0)
        ]
        x, y = lax.shift_right_logical(self.me_s, 1), self.me_s & 1
        at_start = self.me_t == 0

        def turn(x, y):
            first = at_start & (x + y == 0)
            return jnp.where(first, self.sta_count, y * self.x_count + x)

        mine = turn(x, y)
        self.peers, self.later = {(0, 0): self.me_s}, {}
        for dx, dy in self.offsets:
            peer_x, peer_y = (x + dx) & (self.x_count - 1), y ^ dy
            self.peers[dx, dy] = 2 * peer_x + peer_y
            self.later[dx, dy] = turn(peer_x, peer_y) < mine
        self.order = [(0,1),(2,1),(1,1),(3,1),(2,0),(1,0),(3,0),(0,0)]

    def time_device(self, by):
        return self.me_t + by

    def has(self, by):
        return self.me_t + by >= 0 if by < 0 else self.me_t + by < self.tm_count

    def last_to_come(self, by):
        if by > 0:
            return self.me_t == 0
        return self.me_t + by != 0

    def later_peer(self, dx, dy):
        return self.later[dx, dy]

    def station_device(self, dx, dy):
        return self.peers[dx, dy]


def greet(places):
    barrier = pltpu.get_barrier_semaphore()
    for by in (-2, -1, 1, 2):

        @pl.when(places.has(by) & jnp.logical_not(places.last_to_come(by)))
        def _():
            pl.semaphore_signal(
                barrier, inc=1, device_id={"tm": places.time_device(by)}, device_id_type=MESH
            )

    for dx, dy in places.offsets:

        @pl.when(jnp.logical_not(places.later_peer(dx, dy)))
        def _():
            pl.semaphore_signal(
                barrier,
                inc=1,
                device_id={"sta": places.station_device(dx, dy)},
                device_id_type=MESH,
            )


def await_greetings(places):
    near = sum(
        jnp.where(places.has(by) & places.last_to_come(by), 1, 0) for by in (-2, -1, 1, 2)
    )
    far = sum(jnp.where(places.later_peer(dx, dy), 1, 0) for dx, dy in places.offsets)
    barrier = pltpu.get_barrier_semaphore()

    @pl.when(near + far > 0)
    def _():
        pl.semaphore_wait(barrier, near + far)


def answer_near(places, near_sem):
    for by in (-1, 1, 2):

        @pl.when(places.has(by) & places.last_to_come(by))
        def _():
            pl.semaphore_signal(
                near_sem.at[2 - by],
                inc=1,
                device_id={"tm": places.time_device(by)},
                device_id_type=MESH,
            )


def answer_far(places, far_sem):
    for dx, dy in places.offsets:
        back = (-dx % places.x_count, dy)

        @pl.when(places.later_peer(dx, dy))
        def _():
            pl.semaphore_signal(
                far_sem.at[places.offsets.index(back)],
                inc=1,
                device_id={"sta": places.station_device(dx, dy)},
                device_id_type=MESH,
            )


def halo_copies(places, slab, window, halo_send, halo_recv):
    def halo(slot, by, src, dst, width):
        copy = pltpu.make_async_remote_copy(
            src_ref=window.at[:, pl.ds(src, width)],
            dst_ref=window.at[:, pl.ds(dst, width)],
            send_sem=halo_send.at[slot],
            recv_sem=halo_recv.at[slot],
            device_id={"tm": places.time_device(by)},
            device_id_type=MESH,
        )
        return copy, by

    rest = (BLOCKS + 1) * LANE - (LANE + 2 * slab)
    return [
        halo(0, -2, LANE, LANE + 2 * slab, rest),
        halo(1, -1, LANE, LANE + slab, slab),
        halo(2, 1, slab, 0, LANE),
    ]


def start_halo(places, halos, near_sem):
    for copy, by in halos:
        pl.when(places.has(by) & places.last_to_come(by))(copy.start)
    for copy, by in halos:

        @pl.when(places.has(by) & jnp.logical_not(places.last_to_come(by)))
        def _():
            pl.semaphore_wait(near_sem.at[2 + by], 1)
            copy.start()


def await_halo(places, halos):
    for copy, by in halos:
        pl.when(places.has(-by))(copy.wait_recv)


def finish_halo(places, halos):
    for copy, by in halos:
        pl.when(places.has(by))(copy.wait_send)


def prepare_template(values):
    values = values.astype(jnp.float32)
    mean = jnp.sum(values, axis=0, keepdims=True) * (1.0 / TLEN)
    centred = values - mean
    power = jnp.sum(centred * centred, axis=0, keepdims=True) * (1.0 / TLEN)
    factor = lax.rsqrt(power + 1e-06) * (1.0 / math.sqrt(TLEN))
    scaled = centred * factor
    groups = scaled.reshape(TLEN // 8, 8, values.shape[1])
    back = 7 - lax.broadcasted_iota(jnp.int32, groups.shape, 1)
    reversed_groups = jnp.take_along_axis(groups, back, axis=1, mode="promise_in_bounds")
    return jnp.transpose(reversed_groups.reshape(scaled.shape)).astype(jnp.bfloat16)


def store_in_order(places, share, rows, ref):
    order = [places.station_device(dx, dy) for dx, dy in places.order]
    for block in range(places.sta_count):
        slot = sum(jnp.where(peer == block, i, 0) for i, peer in enumerate(order))
        start = pl.multiple_of(slot * share, share)
        ref[pl.ds(start, share), :] = rows[share * block : share * (block + 1)]


def prepare_templates(places, share, raw_templates, unit):
    for c in range(unit.shape[0]):
        store_in_order(places, share, prepare_template(raw_templates[c]), unit.at[c])


def bandpass(places, slab, window, bands):
    first = jnp.where(places.me_t == 0, 0.0, window[:, 0:LANE])
    raw = [first] + [window[:, LANE * b : LANE * (b + 1)] for b in range(1, BLOCKS + 1)]
    lows = jnp.concatenate(raw[:BLOCKS], axis=0)
    highs = jnp.concatenate(raw[1:], axis=0)
    filtered = jnp.dot(
        jnp.concatenate([lows, highs], axis=1),
        bands,
        precision=lax.Precision.HIGHEST,
        preferred_element_type=jnp.float32,
    )
    remaining = (places.tm_count - places.me_t) * slab
    return [
        jnp.where(b * LANE < remaining, filtered[8 * b : 8 * b + 8], 0.0) for b in range(BLOCKS)
    ]


def window_bands():
    row = lax.broadcasted_iota(jnp.int32, (5 * LANE, LANE), 0)
    lane = lax.broadcasted_iota(jnp.int32, (5 * LANE, LANE), 1)
    ahead = row - lane
    return jnp.where((ahead >= 0) & (ahead < TLEN), 1.0, 0.0).astype(jnp.bfloat16)


def window_norm(blocks, mask):
    padded = blocks + [jnp.zeros((8, LANE), jnp.float32)]
    both = [jnp.concatenate([block, block * block], axis=0) for block in padded]
    pieces = []
    for _ in range(3):
        rounded = [block.astype(jnp.bfloat16) for block in both]
        both = [block - part.astype(jnp.float32) for block, part in zip(both, rounded)]
        pieces += [jnp.concatenate(rounded[b : b + 5], axis=1) for b in range(8)]
    sums = jnp.dot(
        jnp.concatenate(pieces, axis=0), window_bands(), preferred_element_type=jnp.float32
    )
    sums = (sums[256:384] + sums[128:256]) + sums[0:128]
    window_sum = jnp.concatenate([sums[16 * b : 16 * b + 8] for b in range(8)], axis=1)
    window_power = jnp.concatenate([sums[16 * b + 8 : 16 * b + 16] for b in range(8)], axis=1)
    inverse_norm = lax.rsqrt(
        jnp.maximum(window_power - window_sum * window_sum * (1.0 / TLEN), 1.0)
    )
    row = lax.broadcasted_iota(jnp.int32, (8, 8 * LANE), 0)
    return inverse_norm * jnp.where(row < 3, mask[0], mask[1]).astype(jnp.float32)


def build_hankel(blocks, hankel):
    lane = lax.broadcasted_iota(jnp.int32, (8, LANE), 1)
    line = lax.broadcasted_iota(jnp.int32, (8, LANE), 0)
    for c in range(hankel.shape[0]):
        rows = [jnp.broadcast_to(blocks[b][c : c + 1], (8, LANE)) for b in range(BLOCKS)]
        for g in range(0, 16, 2):
            halves = []
            for h in (g, g + 1):
                turned = [pltpu.roll(row, 121 - 8 * h, 1, stride=1, stride_axis=0) for row in rows]
                turned.append(jnp.zeros((8, LANE), jnp.float32))
                inside = lane + (8 * h + 7) - line < LANE
                halves.append(
                    [jnp.where(inside, turned[b], turned[b + 1]) for b in range(BLOCKS)]
                )
            for b in range(BLOCKS):
                hankel[c, 8 * g : 8 * g + 16, LANE * b : LANE * (b + 1)] = jnp.concatenate(
                    [halves[0][b], halves[1][b]], axis=0
                ).astype(jnp.bfloat16)


def correlate(c, rows, unit, hankel):
    matrix = jnp.concatenate(
        [
            hankel[c, 0 : min(LANE, TLEN - LANE * m), LANE * m : LANE * (m + 8)]
            for m in range(4)
        ],
        axis=0,
    )
    return jnp.dot(rows, matrix, preferred_element_type=jnp.float32)


def moved(products, inverse_norm, delay):
    rows = products.shape[0]
    lane = lax.broadcasted_iota(jnp.int32, (rows, LANE), 1)
    by_256 = delay >= 256
    by_128 = lax.rem(delay, 256) >= 128
    fine = lax.rem(delay, 128)
    p = [
        products[:, LANE * b : LANE * (b + 1)] * inverse_norm[:, LANE * b : LANE * (b + 1)]
        for b in range(8)
    ]
    p = [jnp.where(by_256, p[b + 2], p[b]) for b in range(6)]
    p = [jnp.where(by_128, p[b + 1], p[b]) for b in range(5)]
    source = lax.rem(lane + fine, LANE)
    ahead = lane < fine
    return [
        jnp.take_along_axis(
            jnp.where(ahead, p[b + 1], p[b]), source, axis=1, mode="promise_in_bounds"
        )
        for b in range(4)
    ]


def match(first, count, delays, inverse_norm, unit, hankel, partial):
    total = None
    for c in range(unit.shape[0]):
        products = correlate(c, unit[c, first : first + count, :], unit, hankel)
        delay = jnp.broadcast_to(delays[first : first + count, c : c + 1], (count, LANE))
        terms = moved(products, inverse_norm[c : c + 1], delay)
        total = terms if total is None else [a + b for a, b in zip(total, terms)]
    for b in range(4):
        partial[first : first + count, LANE * b : LANE * (b + 1)] = total[b]


def send_sum(places, share, slot, partial, received, far_sem, sum_send, sum_recv):
    offset = places.order[slot]

    @pl.when(jnp.logical_not(places.later_peer(*offset)))
    def _():
        pl.semaphore_wait(far_sem.at[places.offsets.index(offset)], 1)

    copy = pltpu.make_async_remote_copy(
        src_ref=partial.at[pl.ds(share * slot, share)],
        dst_ref=received.at[slot],
        send_sem=sum_send.at[slot],
        recv_sem=sum_recv.at[slot],
        device_id={"sta": places.station_device(*offset)},
        device_id_type=MESH,
    )
    copy.start()
    return copy


def add_received(places, share, copies, partial, received, out_ref):
    result = partial[share * len(copies) :, :]
    for slot, copy in enumerate(copies):
        copy.wait_recv()
        result = result + received[slot]
    out_ref[...] = result
    for copy in copies:
        copy.wait_send()


def kernel(
    sizes,
    traces_ref,
    taps_ref,
    templates_ref,
    moveouts_ref,
    mask_ref,
    out_ref,
    samples,
    taps,
    moveouts,
    mask,
    window,
    raw_templates,
    unit,
    delays,
    hankel,
    partial,
    received,
    near_sem,
    far_sem,
    local_sem,
    halo_send,
    halo_recv,
    sum_send,
    sum_recv,
):
    slab, channels, share = sizes[2:]
    kcount = share * sizes[1]
    places = Places(sizes)
    fetches = [
        pltpu.make_async_copy(src, dst, local_sem.at[i])
        for i, (src, dst) in enumerate(
            [(traces_ref, samples), (taps_ref, taps), (moveouts_ref, moveouts), (mask_ref, mask)]
            + [(templates_ref.at[c], raw_templates.at[c]) for c in range(channels)]
        )
    ]
    for fetch in fetches:
        fetch.start()
    window[...] = jnp.zeros_like(window)
    greet(places)
    await_greetings(places)
    answer_near(places, near_sem)
    fetches[0].wait()
    window[0:channels, LANE : LANE + slab] = samples[...]
    halos = halo_copies(places, slab, window, halo_send, halo_recv)
    start_halo(places, halos, near_sem)
    answer_far(places, far_sem)
    fetches[1].wait()
    bands = toeplitz(taps[...])
    fetches[2].wait()
    turned = jnp.transpose(
        jnp.concatenate([moveouts[...], jnp.zeros((8 - channels, kcount), jnp.int32)], axis=0)
    )
    store_in_order(places, share, turned, delays)
    for fetch in fetches[3:]:
        fetch.wait()
    prepare_templates(places, share, raw_templates, unit)
    await_halo(places, halos)
    blocks = bandpass(places, slab, window, bands)
    inverse_norm = window_norm(blocks, mask)
    build_hankel(blocks, hankel)
    copies = []
    first = 0
    for group in CHUNKS:
        match(first * share, group * share, delays, inverse_norm, unit, hankel, partial)
        for slot in range(first, min(first + group, places.sta_count - 1)):
            copies.append(
                send_sum(places, share, slot, partial, received, far_sem, sum_send, sum_recv)
            )
        first += group
    add_received(places, share, copies, partial, received, out_ref)
    finish_halo(places, halos)


def per_device(sizes, traces, taps, templates, moveouts, mask):
    tm_count, sta_count, slab, channels, share = sizes
    kcount = share * sta_count
    vmem = pl.BlockSpec(memory_space=pltpu.VMEM)
    hbm = pl.BlockSpec(memory_space=pltpu.HBM)
    return pl.pallas_call(
        functools.partial(kernel, sizes),
        out_shape=jax.ShapeDtypeStruct((share, slab), jnp.float32),
        in_specs=[hbm] * 5,
        out_specs=vmem,
        scratch_shapes=[
            pltpu.VMEM((channels, slab), jnp.float32),
            pltpu.VMEM((1, LANE), jnp.float32),
            pltpu.VMEM((channels, kcount), jnp.int32),
            pltpu.SMEM((2,), jnp.int32),
            pltpu.VMEM((8, (BLOCKS + 1) * LANE), jnp.float32),
            pltpu.VMEM((channels, TLEN, kcount), jnp.bfloat16),
            pltpu.VMEM((channels, kcount, TLEN), jnp.bfloat16),
            pltpu.VMEM((kcount, 8), jnp.int32),
            pltpu.VMEM((channels, LANE, BLOCKS * LANE), jnp.bfloat16),
            pltpu.VMEM((kcount, slab), jnp.float32),
            pltpu.VMEM((sta_count - 1, share, slab), jnp.float32),
            pltpu.SemaphoreType.REGULAR((5,)),
            pltpu.SemaphoreType.REGULAR((sta_count - 1,)),
            pltpu.SemaphoreType.DMA((4 + channels,)),
            pltpu.SemaphoreType.DMA((3,)),
            pltpu.SemaphoreType.DMA((3,)),
            pltpu.SemaphoreType.DMA((sta_count - 1,)),
            pltpu.SemaphoreType.DMA((sta_count - 1,)),
        ],
        compiler_params=pltpu.CompilerParams(
            collective_id=0, has_side_effects=True, vmem_limit_bytes=24 * 2**20
        ),
        cost_estimate=pl.CostEstimate(
            flops=2 * kcount * channels * 512 * 1024, bytes_accessed=4 * 2**20, transcendentals=0
        ),
        name="network_match",
    )(
        *(
            pltpu.with_memory_space_constraint(array, pltpu.HBM)
            for array in (
                traces,
                taps.reshape(1, LANE),
                jnp.transpose(templates, (1, 2, 0)),
                jnp.transpose(moveouts),
                mask,
            )
        )
    )


def solution(mesh):
    tm_count, sta_count = mesh.shape["tm"], mesh.shape["sta"]

    def run(traces, taps, templates, moveouts, mask):
        sizes = (
            tm_count,
            sta_count,
            traces.shape[1] // tm_count,
            traces.shape[0] // sta_count,
            templates.shape[0] // sta_count,
        )
        return jax.shard_map(
            functools.partial(per_device, sizes),
            mesh=mesh,
            in_specs=(P("sta", "tm"), P(), P(None, "sta", None), P(None, "sta"), P("sta")),
            out_specs=P("sta", "tm"),
            check_vma=False,
        )(traces, taps, templates, moveouts, mask)

    return run
```

```python
import functools
import math

import jax
import jax.numpy as jnp
from jax import lax
from jax.experimental import pallas as pl
from jax.experimental.pallas import tpu as pltpu
from jax.sharding import PartitionSpec as P

TLEN = 400
DMAX = 400
LANE = 128
BLOCKS = 11
CHUNKS = (4, 4)
MESH = pl.DeviceIdType.MESH


def shifted_left(values, step):
    extent = values.shape[-1]
    if step % LANE == 0:
        return jnp.concatenate([values[:, step:], values[:, :step]], axis=1)
    return pltpu.roll(values, extent - step, 1)


def toeplitz(taps):
    rows = jnp.broadcast_to(taps, (LANE, LANE))
    turned = pltpu.roll(rows, 0, 1, stride=1, stride_axis=0)
    row = lax.broadcasted_iota(jnp.int32, (LANE, LANE), 0)
    lane = lax.broadcasted_iota(jnp.int32, (LANE, LANE), 1)
    below = jnp.where(lane >= row, turned, 0.0)
    above = jnp.where(lane < row, turned, 0.0)
    return jnp.concatenate([above, below], axis=0)


def position():
    return lax.axis_index("tm"), lax.axis_index("sta")


class Places:
    def __init__(self, sizes):
        self.tm_count, self.sta_count = sizes[0], sizes[1]
        self.x_count = self.sta_count // 2
        self.me_t, self.me_s = position()
        self.offsets = [
            (dx, dy) for dx in range(self.x_count) for dy in range(2) if (dx, dy) != (0, 0)
        ]
        x, y = lax.shift_right_logical(self.me_s, 1), self.me_s & 1
        at_start = self.me_t == 0

        def turn(x, y):
            first = at_start & (x + y == 0)
            return jnp.where(first, self.sta_count, y * self.x_count + x)

        mine = turn(x, y)
        self.peers, self.later = {(0, 0): self.me_s}, {}
        for dx, dy in self.offsets:
            peer_x, peer_y = (x + dx) & (self.x_count - 1), y ^ dy
            self.peers[dx, dy] = 2 * peer_x + peer_y
            self.later[dx, dy] = turn(peer_x, peer_y) < mine
        self.order = [(0,1),(2,1),(1,1),(3,1),(2,0),(1,0),(3,0),(0,0)]

    def time_device(self, by):
        return self.me_t + by

    def has(self, by):
        return self.me_t + by >= 0 if by < 0 else self.me_t + by < self.tm_count

    def last_to_come(self, by):
        if by > 0:
            return self.me_t == 0
        return self.me_t + by != 0

    def later_peer(self, dx, dy):
        return self.later[dx, dy]

    def station_device(self, dx, dy):
        return self.peers[dx, dy]


def greet(places):
    barrier = pltpu.get_barrier_semaphore()
    for by in (-2, -1, 1, 2):

        @pl.when(places.has(by) & jnp.logical_not(places.last_to_come(by)))
        def _():
            pl.semaphore_signal(
                barrier, inc=1, device_id={"tm": places.time_device(by)}, device_id_type=MESH
            )

    for dx, dy in places.offsets:

        @pl.when(jnp.logical_not(places.later_peer(dx, dy)))
        def _():
            pl.semaphore_signal(
                barrier,
                inc=1,
                device_id={"sta": places.station_device(dx, dy)},
                device_id_type=MESH,
            )


def await_greetings(places):
    near = sum(
        jnp.where(places.has(by) & places.last_to_come(by), 1, 0) for by in (-2, -1, 1, 2)
    )
    far = sum(jnp.where(places.later_peer(dx, dy), 1, 0) for dx, dy in places.offsets)
    barrier = pltpu.get_barrier_semaphore()

    @pl.when(near + far > 0)
    def _():
        pl.semaphore_wait(barrier, near + far)


def answer_near(places, near_sem):
    for by in (-1, 1, 2):

        @pl.when(places.has(by) & places.last_to_come(by))
        def _():
            pl.semaphore_signal(
                near_sem.at[2 - by],
                inc=1,
                device_id={"tm": places.time_device(by)},
                device_id_type=MESH,
            )


def answer_far(places, far_sem):
    for dx, dy in places.offsets:
        back = (-dx % places.x_count, dy)

        @pl.when(places.later_peer(dx, dy))
        def _():
            pl.semaphore_signal(
                far_sem.at[places.offsets.index(back)],
                inc=1,
                device_id={"sta": places.station_device(dx, dy)},
                device_id_type=MESH,
            )


def halo_copies(places, slab, window, halo_send, halo_recv):
    def halo(slot, by, src, dst, width):
        copy = pltpu.make_async_remote_copy(
            src_ref=window.at[:, pl.ds(src, width)],
            dst_ref=window.at[:, pl.ds(dst, width)],
            send_sem=halo_send.at[slot],
            recv_sem=halo_recv.at[slot],
            device_id={"tm": places.time_device(by)},
            device_id_type=MESH,
        )
        return copy, by

    rest = (BLOCKS + 1) * LANE - (LANE + 2 * slab)
    return [
        halo(0, -2, LANE, LANE + 2 * slab, rest),
        halo(1, -1, LANE, LANE + slab, slab),
        halo(2, 1, slab, 0, LANE),
    ]


def start_halo(places, halos, near_sem):
    for copy, by in halos:
        pl.when(places.has(by) & places.last_to_come(by))(copy.start)
    for copy, by in halos:

        @pl.when(places.has(by) & jnp.logical_not(places.last_to_come(by)))
        def _():
            pl.semaphore_wait(near_sem.at[2 + by], 1)
            copy.start()


def await_halo(places, halos):
    for copy, by in halos:
        pl.when(places.has(-by))(copy.wait_recv)


def finish_halo(places, halos):
    for copy, by in halos:
        pl.when(places.has(by))(copy.wait_send)


def prepare_template(values):
    values = values.astype(jnp.float32)
    mean = jnp.sum(values, axis=0, keepdims=True) * (1.0 / TLEN)
    centred = values - mean
    power = jnp.sum(centred * centred, axis=0, keepdims=True) * (1.0 / TLEN)
    factor = lax.rsqrt(power + 1e-06) * (1.0 / math.sqrt(TLEN))
    scaled = centred * factor
    groups = scaled.reshape(TLEN // 8, 8, values.shape[1])
    back = 7 - lax.broadcasted_iota(jnp.int32, groups.shape, 1)
    reversed_groups = jnp.take_along_axis(groups, back, axis=1, mode="promise_in_bounds")
    return jnp.transpose(reversed_groups.reshape(scaled.shape)).astype(jnp.bfloat16)


def store_in_order(places, share, rows, ref):
    order = [places.station_device(dx, dy) for dx, dy in places.order]
    for block in range(places.sta_count):
        slot = sum(jnp.where(peer == block, i, 0) for i, peer in enumerate(order))
        start = pl.multiple_of(slot * share, share)
        ref[pl.ds(start, share), :] = rows[share * block : share * (block + 1)]


def prepare_templates(places, share, raw_templates, unit):
    for c in range(unit.shape[0]):
        store_in_order(places, share, prepare_template(raw_templates[c]), unit.at[c])


def bandpass(places, slab, window, bands):
    first = jnp.where(places.me_t == 0, 0.0, window[:, 0:LANE])
    raw = [first] + [window[:, LANE * b : LANE * (b + 1)] for b in range(1, BLOCKS + 1)]
    lows = jnp.concatenate(raw[:BLOCKS], axis=0)
    highs = jnp.concatenate(raw[1:], axis=0)
    filtered = jnp.dot(
        jnp.concatenate([lows, highs], axis=1),
        bands,
        precision=lax.Precision.HIGHEST,
        preferred_element_type=jnp.float32,
    )
    remaining = (places.tm_count - places.me_t) * slab
    return [
        jnp.where(b * LANE < remaining, filtered[8 * b : 8 * b + 8], 0.0) for b in range(BLOCKS)
    ]


def window_bands():
    row = lax.broadcasted_iota(jnp.int32, (5 * LANE, LANE), 0)
    lane = lax.broadcasted_iota(jnp.int32, (5 * LANE, LANE), 1)
    ahead = row - lane
    return jnp.where((ahead >= 0) & (ahead < TLEN), 1.0, 0.0).astype(jnp.bfloat16)


def window_norm(blocks, mask):
    padded = blocks + [jnp.zeros((8, LANE), jnp.float32)]
    both = [jnp.concatenate([block, block * block], axis=0) for block in padded]
    pieces = []
    for _ in range(3):
        rounded = [block.astype(jnp.bfloat16) for block in both]
        both = [block - part.astype(jnp.float32) for block, part in zip(both, rounded)]
        pieces += [jnp.concatenate(rounded[b : b + 5], axis=1) for b in range(8)]
    sums = jnp.dot(
        jnp.concatenate(pieces, axis=0), window_bands(), preferred_element_type=jnp.float32
    )
    sums = (sums[256:384] + sums[128:256]) + sums[0:128]
    window_sum = jnp.concatenate([sums[16 * b : 16 * b + 8] for b in range(8)], axis=1)
    window_power = jnp.concatenate([sums[16 * b + 8 : 16 * b + 16] for b in range(8)], axis=1)
    inverse_norm = lax.rsqrt(
        jnp.maximum(window_power - window_sum * window_sum * (1.0 / TLEN), 1.0)
    )
    row = lax.broadcasted_iota(jnp.int32, (8, 8 * LANE), 0)
    return inverse_norm * jnp.where(row < 3, mask[0], mask[1]).astype(jnp.float32)


def build_hankel(blocks, hankel):
    lane = lax.broadcasted_iota(jnp.int32, (8, LANE), 1)
    line = lax.broadcasted_iota(jnp.int32, (8, LANE), 0)
    for c in range(hankel.shape[0]):
        rows = [jnp.broadcast_to(blocks[b][c : c + 1], (8, LANE)) for b in range(BLOCKS)]
        for g in range(0, 16, 2):
            halves = []
            for h in (g, g + 1):
                turned = [pltpu.roll(row, 121 - 8 * h, 1, stride=1, stride_axis=0) for row in rows]
                turned.append(jnp.zeros((8, LANE), jnp.float32))
                inside = lane + (8 * h + 7) - line < LANE
                halves.append(
                    [jnp.where(inside, turned[b], turned[b + 1]) for b in range(BLOCKS)]
                )
            for b in range(BLOCKS):
                hankel[c, 8 * g : 8 * g + 16, LANE * b : LANE * (b + 1)] = jnp.concatenate(
                    [halves[0][b], halves[1][b]], axis=0
                ).astype(jnp.bfloat16)


def correlate(c, rows, unit, hankel):
    matrix = jnp.concatenate(
        [
            hankel[c, 0 : min(LANE, TLEN - LANE * m), LANE * m : LANE * (m + 8)]
            for m in range(4)
        ],
        axis=0,
    )
    return jnp.dot(rows, matrix, preferred_element_type=jnp.float32)


def moved(products, inverse_norm, delay):
    rows = products.shape[0]
    lane = lax.broadcasted_iota(jnp.int32, (rows, LANE), 1)
    by_256 = delay >= 256
    by_128 = lax.rem(delay, 256) >= 128
    fine = lax.rem(delay, 128)
    p = [
        products[:, LANE * b : LANE * (b + 1)] * inverse_norm[:, LANE * b : LANE * (b + 1)]
        for b in range(8)
    ]
    p = [jnp.where(by_256, p[b + 2], p[b]) for b in range(6)]
    p = [jnp.where(by_128, p[b + 1], p[b]) for b in range(5)]
    source = lax.rem(lane + fine, LANE)
    ahead = lane < fine
    return [
        jnp.take_along_axis(
            jnp.where(ahead, p[b + 1], p[b]), source, axis=1, mode="promise_in_bounds"
        )
        for b in range(4)
    ]


def match(first, count, delays, inverse_norm, unit, hankel, partial):
    total = None
    for c in range(unit.shape[0]):
        products = correlate(c, unit[c, first : first + count, :], unit, hankel)
        delay = jnp.broadcast_to(delays[first : first + count, c : c + 1], (count, LANE))
        terms = moved(products, inverse_norm[c : c + 1], delay)
        total = terms if total is None else [a + b for a, b in zip(total, terms)]
    for b in range(4):
        partial[first : first + count, LANE * b : LANE * (b + 1)] = total[b]


def send_sum(places, share, slot, partial, received, far_sem, sum_send, sum_recv):
    offset = places.order[slot]

    @pl.when(jnp.logical_not(places.later_peer(*offset)))
    def _():
        pl.semaphore_wait(far_sem.at[places.offsets.index(offset)], 1)

    copy = pltpu.make_async_remote_copy(
        src_ref=partial.at[pl.ds(share * slot, share)],
        dst_ref=received.at[slot],
        send_sem=sum_send.at[slot],
        recv_sem=sum_recv.at[slot],
        device_id={"sta": places.station_device(*offset)},
        device_id_type=MESH,
    )
    copy.start()
    return copy


def add_received(places, share, copies, partial, received, out_ref):
    result = partial[share * len(copies) :, :]
    arrival = sorted(range(len(copies)), key=lambda i: (places.order[i][1], places.order[i] == (2, 1)))
    for slot in arrival:
        copies[slot].wait_recv()
        result = result + received[slot]
    out_ref[...] = result
    for copy in copies:
        copy.wait_send()


def kernel(
    sizes,
    traces_ref,
    taps_ref,
    templates_ref,
    moveouts_ref,
    mask_ref,
    out_ref,
    samples,
    taps,
    moveouts,
    mask,
    window,
    raw_templates,
    unit,
    delays,
    hankel,
    partial,
    received,
    near_sem,
    far_sem,
    local_sem,
    halo_send,
    halo_recv,
    sum_send,
    sum_recv,
):
    slab, channels, share = sizes[2:]
    kcount = share * sizes[1]
    places = Places(sizes)
    fetches = [
        pltpu.make_async_copy(src, dst, local_sem.at[i])
        for i, (src, dst) in enumerate(
            [(traces_ref, samples), (taps_ref, taps), (moveouts_ref, moveouts), (mask_ref, mask)]
            + [(templates_ref.at[c], raw_templates.at[c]) for c in range(channels)]
        )
    ]
    for fetch in fetches:
        fetch.start()
    window[...] = jnp.zeros_like(window)
    greet(places)
    await_greetings(places)
    answer_near(places, near_sem)
    fetches[0].wait()
    window[0:channels, LANE : LANE + slab] = samples[...]
    halos = halo_copies(places, slab, window, halo_send, halo_recv)
    start_halo(places, halos, near_sem)
    answer_far(places, far_sem)
    fetches[1].wait()
    bands = toeplitz(taps[...])
    fetches[2].wait()
    turned = jnp.transpose(
        jnp.concatenate([moveouts[...], jnp.zeros((8 - channels, kcount), jnp.int32)], axis=0)
    )
    store_in_order(places, share, turned, delays)
    for fetch in fetches[3:]:
        fetch.wait()
    prepare_templates(places, share, raw_templates, unit)
    await_halo(places, halos)
    blocks = bandpass(places, slab, window, bands)
    inverse_norm = window_norm(blocks, mask)
    build_hankel(blocks, hankel)
    copies = []
    first = 0
    for group in CHUNKS:
        match(first * share, group * share, delays, inverse_norm, unit, hankel, partial)
        for slot in range(first, min(first + group, places.sta_count - 1)):
            copies.append(
                send_sum(places, share, slot, partial, received, far_sem, sum_send, sum_recv)
            )
        first += group
    add_received(places, share, copies, partial, received, out_ref)
    finish_halo(places, halos)


def per_device(sizes, traces, taps, templates, moveouts, mask):
    tm_count, sta_count, slab, channels, share = sizes
    kcount = share * sta_count
    vmem = pl.BlockSpec(memory_space=pltpu.VMEM)
    hbm = pl.BlockSpec(memory_space=pltpu.HBM)
    return pl.pallas_call(
        functools.partial(kernel, sizes),
        out_shape=jax.ShapeDtypeStruct((share, slab), jnp.float32),
        in_specs=[hbm] * 5,
        out_specs=vmem,
        scratch_shapes=[
            pltpu.VMEM((channels, slab), jnp.float32),
            pltpu.VMEM((1, LANE), jnp.float32),
            pltpu.VMEM((channels, kcount), jnp.int32),
            pltpu.SMEM((2,), jnp.int32),
            pltpu.VMEM((8, (BLOCKS + 1) * LANE), jnp.float32),
            pltpu.VMEM((channels, TLEN, kcount), jnp.bfloat16),
            pltpu.VMEM((channels, kcount, TLEN), jnp.bfloat16),
            pltpu.VMEM((kcount, 8), jnp.int32),
            pltpu.VMEM((channels, LANE, BLOCKS * LANE), jnp.bfloat16),
            pltpu.VMEM((kcount, slab), jnp.float32),
            pltpu.VMEM((sta_count - 1, share, slab), jnp.float32),
            pltpu.SemaphoreType.REGULAR((5,)),
            pltpu.SemaphoreType.REGULAR((sta_count - 1,)),
            pltpu.SemaphoreType.DMA((4 + channels,)),
            pltpu.SemaphoreType.DMA((3,)),
            pltpu.SemaphoreType.DMA((3,)),
            pltpu.SemaphoreType.DMA((sta_count - 1,)),
            pltpu.SemaphoreType.DMA((sta_count - 1,)),
        ],
        compiler_params=pltpu.CompilerParams(
            collective_id=0, has_side_effects=True, vmem_limit_bytes=24 * 2**20
        ),
        cost_estimate=pl.CostEstimate(
            flops=2 * kcount * channels * 512 * 1024, bytes_accessed=4 * 2**20, transcendentals=0
        ),
        name="network_match",
    )(
        *(
            pltpu.with_memory_space_constraint(array, pltpu.HBM)
            for array in (
                traces,
                taps.reshape(1, LANE),
                jnp.transpose(templates, (1, 2, 0)),
                jnp.transpose(moveouts),
                mask,
            )
        )
    )


def solution(mesh):
    tm_count, sta_count = mesh.shape["tm"], mesh.shape["sta"]

    def run(traces, taps, templates, moveouts, mask):
        sizes = (
            tm_count,
            sta_count,
            traces.shape[1] // tm_count,
            traces.shape[0] // sta_count,
            templates.shape[0] // sta_count,
        )
        return jax.shard_map(
            functools.partial(per_device, sizes),
            mesh=mesh,
            in_specs=(P("sta", "tm"), P(), P(None, "sta", None), P(None, "sta"), P("sta")),
            out_specs=P("sta", "tm"),
            check_vma=False,
        )(traces, taps, templates, moveouts, mask)

    return run
```
